32 devices in a mesh: expert: 8 (over z, y), tensor: 4 (over x, core).
Axes of the slice: x: 2, y: 2, z: 4, core: 2. Of those that a mesh axis runs over, the one named last changes fastest.
Arguments:
- hidden: float32 [8192, 2048], P(('expert', 'tensor')), may hold values from -6 to 6
- segments: int32 [8192], P('expert'), may hold values from 0 to 2, as said below
- routes: int32 [8192, 8], P(('expert', 'tensor')), may hold values from 0 to 63, all different within a row; in each aligned block of 256 rows (0 to 255, 256 to 511, ...) at most 48 rows name the same one
- attn_gain: float32 [2048], replicated, may hold values from 0.5 to 1.5
- qkv_weight: bfloat16 [3, 2048, 2048], P(None, None, 'tensor'), may hold values from -0.125 to 0.125
- qk_gain: float32 [2, 2048], P(None, 'tensor'), may hold values from 0.5 to 1.5
- out_weight: bfloat16 [2048, 2048], P('tensor'), may hold values from -0.5 to 0.5
- moe_gain: float32 [2048], replicated, may hold values from 0.5 to 1.5
- router_weight: bfloat16 [2048, 64], replicated, may hold values from -0.06591797 to 0.06591797
- expert_up: bfloat16 [64, 2, 2048, 1024], P('expert', None, None, 'tensor'), may hold values from -0.125 to 0.125
- expert_down: bfloat16 [64, 1024, 2048], P('expert', 'tensor'), may hold values from -3 to 3
- cotangent: float32 [8192, 2048], P(('expert', 'tensor')), may hold values from -6 to 6
Outputs:
- output: float32 [8192, 2048], P(('expert', 'tensor'))
- hidden_grad: float32 [8192, 2048], P(('expert', 'tensor'))
- attn_gain_grad: float32 [2048], replicated
- qkv_grad: float32 [3, 2048, 2048], P(None, None, 'tensor')
- qk_gain_grad: float32 [2, 2048], P(None, 'tensor')
- out_grad: float32 [2048, 2048], P('tensor')
- moe_gain_grad: float32 [2048], replicated
- router_grad: float32 [2048, 64], replicated
- up_grad: float32 [64, 2, 2048, 1024], P('expert', None, None, 'tensor')
- down_grad: float32 [64, 1024, 2048], P('expert', 'tensor')
The draws below stay inside these ranges and needn't reach their ends.
Inputs may be any that keep to these rules, and one draw needn't show every extreme that they name: `segments`: each sequence of 1024 tokens holds three documents, numbered 0, 1, 2 in order; document 1 starts within the first 256 tokens and ends within the last 256. `routes`: in the rows of one device each expert is named by at most 48 rows.
All inputs are finite; a program needn't handle non-finite values.
Results may differ from the reference program's by a relative error of at most 0.019.
Values may be sent and summed in bfloat16 or wider, within the bound.
No kernel may reach another device: no remote copies, remote signals or barrier semaphores. Data moves between devices by JAX's collectives and lax.ppermute only.
A program may use at most 640 MiB of HBM per device.

```python
import math
import jax
import jax.numpy as jnp
import numpy as np
from jax import lax

D = 2048
HEADS = 16
HEAD_DIM = 128
FF = 1024
EXPERTS = 64
TOP = 8
LEN = 1024
TOK_DEV = 256
TOKENS = 8192
CAP = 48


def draw_segments(key, part):
    key = jax.random.fold_in(key, 11)
    count = TOKENS // LEN
    first_key, second_key = jax.random.split(key, 2)
    start = jax.random.randint(first_key, (count, 1), 1, TOK_DEV)
    stop = jax.random.randint(second_key, (count, 1), LEN - TOK_DEV + 1, LEN)
    index = jnp.arange(LEN, dtype=jnp.int32)[None, :]
    numbers = (index >= start).astype(jnp.int32) + (index >= stop).astype(jnp.int32)
    return numbers.reshape(-1).astype(jnp.int32)


def block_levels(own_key, extent, cuts, least, top_value):
    def one(axis_at, blocks):
        heights = jax.random.uniform(jax.random.fold_in(jax.random.fold_in(own_key, 6), axis_at), (blocks,), jnp.float32, least / len(cuts), top_value / len(cuts))
        return jnp.repeat(jnp.exp(heights), extent[axis_at] // blocks).reshape((-1,) + (1,) * (len(extent) - axis_at - 1))

    factor_of = one(*cuts[0])
    for cut in cuts[1:]:
        factor_of = factor_of * one(*cut)
    return factor_of


def deal_out(own_key, own, number, rows, number_of, top, limit, skew):
    sequence = jax.random.permutation(own_key, number_of)
    heavy_load, common = shares(number_of, rows * top, limit, skew, True), shares(number_of, rows * top, limit, skew, False)
    places = jnp.arange(number_of)

    def named(lengths, turn):
        used = int((lengths > 0).sum())
        fixed = max(1, used // 4)
        shifted = fixed + (places - fixed + turn * (used - fixed)) % max(1, number_of - fixed)
        return jnp.zeros((number_of,), jnp.int32).at[sequence[jnp.where(places < fixed, places, shifted)]].set(jnp.asarray(lengths, jnp.int32))

    lengths = jnp.where(number % 4 == 0, named(heavy_load, number // 4), named(common, number - number // 4 - 1))
    mixed = jax.random.permutation(jax.random.fold_in(own, 3), number_of)
    source_of, sink = mixed[0:number_of // 2 * 2:2], mixed[1:number_of // 2 * 2:2]
    slack = jnp.minimum(lengths[source_of] - 1, limit - lengths[sink]) // 2
    slack = jnp.where((source_of == sequence[0]) | (sink == sequence[0]) | (lengths[sink] == 0), 0, jnp.maximum(slack, 0))
    shifted = jax.random.randint(jax.random.fold_in(own, 4), (number_of // 2,), 0, 1 << 20) % (slack + 1)
    lengths = lengths.at[source_of].add(-shifted).at[sink].add(shifted)
    labels = jnp.searchsorted(jnp.cumsum(lengths), jnp.arange(rows * top), side="right").astype(jnp.int32)
    listing = labels.reshape(top, rows).T
    listing = listing[jax.random.permutation(jax.random.fold_in(own, 1), rows)]
    turn = jax.random.randint(jax.random.fold_in(own, 2), (rows, 1), 0, top)
    return jnp.take_along_axis(listing, (jnp.arange(top)[None, :] + turn) % top, axis=1)


def shares(amount, total, most, skew, full):
    portions = [(1 << 20) // math.isqrt(standing ** skew) + 1 for standing in range(1, amount + 1)]
    largest = most if full else min(most, max(-(-total // amount), total * portions[0] // sum(portions)))
    least = 1 if total - largest >= amount - 1 else 0
    given, rest = [largest] + [least] * (amount - 1), total - largest - least * (amount - 1)
    while rest > 0:
        candidates = [i for i in range(1, amount) if given[i] < largest] or [i for i in range(1, amount) if given[i] < most]
        pool, left = sum([portions[i] for i in candidates]), rest
        for i in candidates:
            addition = min(most - given[i], max(1, left * portions[i] // pool), rest)
            given[i] = given[i] + addition
            rest = rest - addition
    return np.array(given)


def gaussian(key, shape, scale, reach, shards=(), held_as=jnp.bfloat16):
    values = scale * jax.random.normal(key, shape, jnp.float32)
    if shards:
        values = values * block_levels(key, shape, shards, -0.22, 0.18)
    return jnp.clip(values, -reach, reach).astype(held_as)


def setup_inputs(seed: int = 0) -> dict:
    streams_of = jax.random.split(jax.random.key(seed), 13)
    hidden = gaussian(streams_of[0], (TOKENS, D), 1.0, 6.0, ((0, 32),), jnp.float32)
    segments = draw_segments(jax.random.fold_in(streams_of[12], 71), 0)
    routes_keys = jax.random.split(jax.random.fold_in(streams_of[2], 1), TOKENS // TOK_DEV)
    routes_turns = jax.random.permutation(jax.random.fold_in(streams_of[2], 3), TOKENS // TOK_DEV)
    routes = jax.vmap(lambda own, number: deal_out(jax.random.fold_in(streams_of[2], 2), own, number, TOK_DEV, EXPERTS, TOP, CAP, 1))(routes_keys, routes_turns).reshape((TOKENS, TOP))
    attn_gain = jnp.clip(1.0 + 0.1 * jax.random.normal(streams_of[3], (D,), jnp.float32), 0.5, 1.5)
    qkv_weight = gaussian(streams_of[4], (3, D, HEADS * HEAD_DIM), D ** -0.5, 0.125, ((2, 4),))
    qk_gain = jnp.clip(1.0 + 0.1 * jax.random.normal(streams_of[5], (2, HEADS * HEAD_DIM), jnp.float32), 0.5, 1.5)
    out_weight = gaussian(streams_of[6], (HEADS * HEAD_DIM, D), (HEADS * HEAD_DIM // 16) ** -0.5, 0.5, ((0, 4),))
    moe_gain = jnp.clip(1.0 + 0.1 * jax.random.normal(streams_of[7], (D,), jnp.float32), 0.5, 1.5)
    router_weight = gaussian(streams_of[8], (D, EXPERTS), (0.5 * D ** -0.5), 0.06591797)
    expert_up = gaussian(streams_of[9], (EXPERTS, 2, D, FF), D ** -0.5, 0.125, ((0, 8), (3, 4)))
    expert_down = gaussian(streams_of[10], (EXPERTS, FF, D), (max(1, FF // 256)) ** -0.5, 3.0, ((0, 8), (1, 4)))
    cotangent = gaussian(streams_of[11], (TOKENS, D), 1.0, 6.0, ((0, 32),), jnp.float32)
    return {"hidden": hidden, "segments": segments, "routes": routes, "attn_gain": attn_gain, "qkv_weight": qkv_weight, "qk_gain": qk_gain, "out_weight": out_weight, "moe_gain": moe_gain, "router_weight": router_weight, "expert_up": expert_up, "expert_down": expert_down, "cotangent": cotangent}


EPSILON = 1e-05
THETA = 10000.0
HIGHEST = lax.Precision.HIGHEST

@jax.custom_vjp
def low(v):
    return lax.optimization_barrier(v.astype(jnp.bfloat16)).astype(jnp.float32)

@jax.custom_vjp
def low_back(v):
    return v

def low_keep(v):
    return (low(v), None)

def low_pass(kept, grad):
    return (grad,)

def back_keep(v):
    return (v, None)

def back_low(kept, grad):
    return (low(grad),)
low.defvjp(low_keep, low_pass)
low_back.defvjp(back_keep, back_low)

def normalize(values, gain):
    return values * lax.rsqrt(lax.optimization_barrier(jnp.mean(values * values, axis=-1, keepdims=True)) + EPSILON) * gain

def doc_positions(segment_ids):
    index = jnp.arange(segment_ids.shape[0], dtype=jnp.int32)
    starts = jnp.concatenate([jnp.ones((1,), jnp.bool_), segment_ids[1:] != segment_ids[:-1]])
    first = lax.cummax(jnp.where(starts, index, 0), axis=0)
    return index - first

def rope_tables(positions, half):
    freq = jnp.exp(-math.log(THETA) * jnp.arange(half, dtype=jnp.float32) / half)
    angle = positions.astype(jnp.float32)[:, None] * freq[None, :]
    return (jnp.cos(angle)[:, None, :], jnp.sin(angle)[:, None, :])

def rotate(values, cosine, sine):
    half = values.shape[-1] // 2
    first = values[..., :half]
    second = values[..., half:]
    return jnp.concatenate([first * cosine - second * sine, second * cosine + first * sine], axis=-1)

def attend(inputs):
    queries, keys_in, values, segment_ids = inputs
    scores = low_back(jnp.einsum('qhd,khd->hqk', queries, keys_in, precision=HIGHEST) * HEAD_DIM ** (-0.5))
    index = jnp.arange(segment_ids.shape[0], dtype=jnp.int32)
    allowed = (segment_ids[:, None] == segment_ids[None, :]) & (index[:, None] >= index[None, :])
    masked = jnp.where(allowed[None], scores, -1e+30)
    top = lax.optimization_barrier(jnp.max(masked, axis=-1, keepdims=True))
    total = jnp.log(lax.optimization_barrier(jnp.sum(jnp.exp(masked - top), axis=-1, keepdims=True))) + top
    probs = low(jnp.exp(masked - total))
    return jnp.einsum('hqk,khd->qhd', probs, values, precision=HIGHEST)

def expert_block(inputs):
    rows, up_pair, down = inputs
    gate = low_back(jnp.dot(rows, up_pair[0], precision=HIGHEST))
    upper = low_back(jnp.dot(rows, up_pair[1], precision=HIGHEST))
    active = low(jax.nn.silu(gate) * upper)
    return low_back(low(jnp.dot(active, down, precision=HIGHEST)))

def slot_rows(routes):
    flat = routes.reshape(-1)
    onehot = (flat[:, None] == jnp.arange(EXPERTS, dtype=jnp.int32)[None, :]).astype(jnp.int32)
    onehot = onehot.reshape(-1, TOK_DEV * TOP, EXPERTS)
    before = jnp.cumsum(onehot, axis=1) - onehot
    rank = lax.optimization_barrier(jnp.sum(before * onehot, axis=-1)).reshape(-1)
    block = jnp.arange(flat.shape[0], dtype=jnp.int32) // (TOK_DEV * TOP)
    return flat * (TOKENS // TOK_DEV * CAP) + block * CAP + rank

def forward(hidden, attn_gain, qkv_weight, qk_gain, out_weight, moe_gain, router_weight, expert_up, expert_down, segments, routes):
    tokens, width = hidden.shape
    normed = low(normalize(hidden, attn_gain))
    projected = low_back(jnp.einsum('td,cdf->ctf', normed, qkv_weight, precision=HIGHEST))
    head_shape = (tokens, HEADS, HEAD_DIM)
    gains = qk_gain.reshape(2, HEADS, HEAD_DIM)
    positions = jax.vmap(doc_positions)(segments.reshape(-1, LEN)).reshape(-1)
    cosine, sine = rope_tables(positions, HEAD_DIM // 2)
    queries = low(rotate(normalize(projected[0].reshape(head_shape), gains[0]), cosine, sine))
    keys_in = low(rotate(normalize(projected[1].reshape(head_shape), gains[1]), cosine, sine))
    values = low(projected[2].reshape(head_shape))
    seq_shape = (-1, LEN, HEADS, HEAD_DIM)
    mixed = lax.map(jax.checkpoint(attend), (queries.reshape(seq_shape), keys_in.reshape(seq_shape), values.reshape(seq_shape), segments.reshape(-1, LEN)))
    mixed = low(low_back(mixed.reshape(tokens, HEADS * HEAD_DIM)))
    attended = hidden + low_back(jnp.dot(mixed, out_weight, precision=HIGHEST))
    routed = low(normalize(attended, moe_gain))
    logits = low_back(jnp.dot(routed, router_weight, precision=HIGHEST))
    probs = jax.nn.softmax(logits, axis=-1)
    gates = jnp.take_along_axis(probs, routes, axis=1)
    slots = slot_rows(routes)
    copies = low_back(jnp.repeat(routed, TOP, axis=0))
    buffer = jnp.zeros((EXPERTS * (TOKENS // TOK_DEV) * CAP, width), jnp.float32).at[slots].set(copies)
    outputs = lax.map(jax.checkpoint(expert_block), (buffer.reshape(EXPERTS, -1, width), expert_up, expert_down))
    returned = outputs.reshape(-1, width)[slots].reshape(tokens, TOP, width)
    return attended + lax.optimization_barrier(jnp.sum(gates[:, :, None] * returned, axis=1))

def reference(hidden, segments, routes, attn_gain, qkv_weight, qk_gain, out_weight, moe_gain, router_weight, expert_up, expert_down, cotangent):
    primals = tuple((array.astype(jnp.float32) for array in (hidden, attn_gain, qkv_weight, qk_gain, out_weight, moe_gain, router_weight, expert_up, expert_down)))

    def layer(*weights):
        return forward(*weights, segments, routes)
    output, pullback = jax.vjp(layer, *primals)
    grads = pullback(cotangent.astype(jnp.float32))
    return (output, grads[0], grads[1], grads[2], grads[3], grads[4], grads[5], grads[6], grads[7], grads[8])
```

```python
import functools
import math

import jax
import jax.numpy as jnp
from jax import lax
from jax.experimental import pallas as pl
from jax.experimental.pallas import tpu as pltpu
from jax.sharding import Mesh, PartitionSpec as P

HEAD_DIM = 128
ALL = ("z", "y", "x", "core")
EXPERT = ("z", "y")
TENSOR = ("x", "core")
LOW = jnp.bfloat16
WIDE = jnp.float32


EPSILON = 1e-05
THETA = 10000.0


def normalize(values, gain):
    inverse = lax.rsqrt(jnp.mean(values * values, axis=-1, keepdims=True) + EPSILON)
    return (values * inverse * gain, inverse)


def norm_back(grad_out, values, inverse, gain):
    scaled = values * inverse
    weighted = grad_out * gain
    grad_in = inverse * (weighted - scaled * jnp.mean(weighted * scaled, axis=-1, keepdims=True))
    return (grad_in, jnp.sum(grad_out * scaled, axis=0))


def doc_positions(segment_ids):
    index = jnp.arange(segment_ids.shape[0], dtype=jnp.int32)
    starts = jnp.concatenate([jnp.ones((1,), jnp.bool_), segment_ids[1:] != segment_ids[:-1]])
    first = lax.cummax(jnp.where(starts, index, 0), axis=0)
    return index - first


def rope_tables(positions, half):
    freq = jnp.exp(-math.log(THETA) * jnp.arange(half, dtype=jnp.float32) / half)
    angle = positions.astype(jnp.float32)[:, None] * freq[None, :]
    return (jnp.cos(angle)[:, None, :], jnp.sin(angle)[:, None, :])


def rotate(values, cosine, sine):
    half = values.shape[-1] // 2
    first = values[..., :half]
    second = values[..., half:]
    return jnp.concatenate(
        [first * cosine - second * sine, second * cosine + first * sine], axis=-1
    )


def add_low(*terms):
    total = terms[0].astype(WIDE)
    for term in terms[1:]:
        total = total + term.astype(WIDE)
    return total.astype(terms[0].dtype)


def swap(values, axis):
    return lax.ppermute(values, axis, [(0, 1), (1, 0)])


def pick(parts, index):
    last = parts.shape[0] - 1
    return lax.dynamic_index_in_dim(parts, jnp.clip(index, 0, last), 0, keepdims=False)


def line_scatter(parts, axis):
    n = lax.axis_size(axis)
    me = lax.axis_index(axis)
    up = down = None
    for step in range(1, n):
        block = pick(parts, me + n - step)
        block = block if up is None else add_low(block, up)
        up = lax.ppermute(block, axis, [(i, i + 1) for i in range(step)])
        block = pick(parts, me - n + step)
        block = block if down is None else add_low(block, down)
        down = lax.ppermute(block, axis, [(i, i - 1) for i in range(n - step, n)])
    return add_low(pick(parts, me), up, down)


def line_gather(values, axis):
    n = lax.axis_size(axis)
    me = lax.axis_index(axis)
    below, above = [], []
    up = down = values
    for step in range(1, n):
        up = lax.ppermute(up, axis, [(i, i + 1) for i in range(step - 1, n - 1)])
        down = lax.ppermute(down, axis, [(i, i - 1) for i in range(1, n - step + 1)])
        below.insert(0, up)
        above.append(down)
    return lax.dynamic_slice_in_dim(jnp.stack(below + [values] + above), n - 1 - me, n, 0)


def relative(axis):
    return lax.axis_size(axis) == 2


def coordinate(axis):
    places = jnp.arange(lax.axis_size(axis), dtype=jnp.int32)
    return places ^ lax.axis_index(axis) if relative(axis) else places


def block_order(axes):
    stride = {}
    step = 1
    for axis in reversed(ALL):
        stride[axis] = step
        step *= lax.axis_size(axis)
    order = jnp.zeros((1,), jnp.int32)
    for axis in axes:
        order = (order[:, None] + coordinate(axis)[None, :] * stride[axis]).reshape(-1)
    return order


def scatter_axis(parts, axis):
    if relative(axis):
        return add_low(parts[0], swap(parts[1], axis))
    return line_scatter(parts, axis)


def scatter_all(keep, send, axes):
    total = add_low(keep, swap(send, "core"))
    for axis in axes:
        total = scatter_axis(total, axis)
    return total


def sum_all(values):
    for axis in ("core", "x", "y", "z"):
        n = lax.axis_size(axis)
        step = 1
        while step < n:
            values = values + lax.ppermute(values, axis, [(i, i ^ step) for i in range(n)])
            step *= 2
    return values


def sum_expert(values):
    rows, columns = values.shape
    ny, nz = lax.axis_size("y"), lax.axis_size("z")
    parts = values.reshape(ny, nz, rows // (ny * nz), columns)
    if relative("y"):
        me = lax.axis_index("y")
        own = add_low(pick(parts, me), swap(pick(parts, 1 - me), "y"))
    else:
        own = line_scatter(parts, "y")
    own = line_gather(line_scatter(own, "z"), "z")
    if relative("y"):
        other = swap(own, "y")
        first = jnp.where(me == 0, own, other)
        second = jnp.where(me == 0, other, own)
        parts = jnp.stack([first, second])
    else:
        parts = line_gather(own, "y")
    return parts.reshape(rows, columns).astype(WIDE)


NT = (((1,), (1,)), ((), ()))
TN = (((0,), (0,)), ((), ()))


def dot(left, right, dims=None):
    if dims is None:
        return jnp.dot(left, right, preferred_element_type=WIDE)
    return lax.dot_general(left, right, dims, preferred_element_type=WIDE)


def params(megabytes):
    return pltpu.CompilerParams(vmem_limit_bytes=megabytes << 20)


def cost(flops, moved):
    return pl.CostEstimate(flops=int(flops), bytes_accessed=int(moved), transcendentals=0)


def dispatch_kernel(order_ref, select_ref, rows_ref, out_ref):
    experts, capacity, width = out_ref.shape
    picked = dot(select_ref[0], rows_ref[0])
    out_ref[...] = picked.astype(LOW).reshape(experts, capacity, width)


def dispatch(order, select, rows, experts):
    blocks, slots, tokens = select.shape
    width = rows.shape[-1]
    capacity = slots // experts
    return pl.pallas_call(
        dispatch_kernel,
        grid_spec=pltpu.PrefetchScalarGridSpec(
            num_scalar_prefetch=1,
            grid=(blocks,),
            in_specs=[
                pl.BlockSpec((1, slots, tokens), lambda b, order: (b, 0, 0)),
                pl.BlockSpec((1, tokens, width), lambda b, order: (order[b], 0, 0)),
            ],
            out_specs=pl.BlockSpec((experts, capacity, width), lambda b, order: (0, b, 0)),
        ),
        out_shape=jax.ShapeDtypeStruct((experts, blocks * capacity, width), LOW),
        compiler_params=params(32),
        cost_estimate=cost(2 * blocks * slots * tokens * width, 2 * blocks * (slots + tokens) * width),
        name="dispatch",
    )(order, select, rows.reshape(blocks, tokens, width))


def row_tile(rows):
    return max(t for t in range(128, 513, 128) if rows % t == 0)


def grad_active_kernel(rows_ref, down_ref, out_ref):
    out_ref[0] = dot(rows_ref[0], down_ref[0], NT)


def grad_active(rows, expert_down):
    experts, count, width = rows.shape
    units = expert_down.shape[1]
    tile = row_tile(count)
    return pl.pallas_call(
        grad_active_kernel,
        grid=(experts, count // tile),
        in_specs=[
            pl.BlockSpec((1, tile, width), lambda e, r: (e, r, 0)),
            pl.BlockSpec((1, units, width), lambda e, r: (e, 0, 0)),
        ],
        out_specs=pl.BlockSpec((1, tile, units), lambda e, r: (e, r, 0)),
        out_shape=jax.ShapeDtypeStruct((experts, count, units), WIDE),
        compiler_params=params(32),
        cost_estimate=cost(2 * rows.size * units, 2 * rows.size),
        name="grad_active",
    )(rows, expert_down)


def hidden_kernel(rows_ref, up_ref, grad_ref, gate_ref, act_ref, pair_ref, gate_grad_ref):
    rows = rows_ref[0]
    gate_pre = dot(rows, up_ref[0, 0])
    upper = dot(rows, up_ref[0, 1])
    gate = gate_ref[0]
    sigma = jax.nn.sigmoid(gate_pre)
    silu = gate_pre * sigma
    active = silu * upper
    grad = grad_ref[0]
    gated = gate * grad
    act_ref[0] = (gate * active).astype(LOW)
    pair_ref[0, 0] = (gated * upper * (sigma * (1.0 + gate_pre * (1.0 - sigma)))).astype(LOW)
    pair_ref[0, 1] = (gated * silu).astype(LOW)
    gate_grad_ref[0] = jnp.sum(active * grad, axis=-1, keepdims=True)


def hidden_units(rows, expert_up, grads, gates):
    experts, count, width = rows.shape
    units = expert_up.shape[-1]
    tile = row_tile(count)
    return pl.pallas_call(
        hidden_kernel,
        grid=(experts, count // tile),
        in_specs=[
            pl.BlockSpec((1, tile, width), lambda e, r: (e, r, 0)),
            pl.BlockSpec((1, 2, width, units), lambda e, r: (e, 0, 0, 0)),
            pl.BlockSpec((1, tile, units), lambda e, r: (e, r, 0)),
            pl.BlockSpec((1, tile, 1), lambda e, r: (e, r, 0)),
        ],
        out_specs=[
            pl.BlockSpec((1, tile, units), lambda e, r: (e, r, 0)),
            pl.BlockSpec((1, 2, tile, units), lambda e, r: (e, 0, r, 0)),
            pl.BlockSpec((1, tile, 1), lambda e, r: (e, r, 0)),
        ],
        out_shape=[
            jax.ShapeDtypeStruct((experts, count, units), LOW),
            jax.ShapeDtypeStruct((experts, 2, count, units), LOW),
            jax.ShapeDtypeStruct((experts, count, 1), WIDE),
        ],
        compiler_params=params(40),
        cost_estimate=cost(4 * rows.size * units, 2 * rows.size),
        name="hidden_units",
    )(rows, expert_up, grads, gates)


def combine_kernel(transposed, experts, lhs_ref, weight_ref, select_ref, keep_ref, send_ref, rows):
    step = pl.program_id(0)
    blocks, slots, columns = rows.shape
    capacity = slots // experts
    group = select_ref.shape[0]
    pairs = lhs_ref.shape[1]
    many = 8

    @pl.when(step < experts)
    def _():
        start = pl.multiple_of(step * capacity, capacity)
        for first in range(0, blocks, many):
            piece = pl.ds(first * capacity, many * capacity)
            total = None
            for i in range(pairs):
                term = dot(lhs_ref[0, i, piece, :], weight_ref[0, i], NT if transposed else None)
                total = term if total is None else total + term
            rows[first : first + many, pl.ds(start, capacity), :] = total.astype(LOW).reshape(
                many, capacity, columns
            )

    @pl.when(step >= experts)
    def _():
        at = (step - experts) * group
        half = (blocks // group) // 2

        def put(ref):
            for i in range(group):
                ref[0, i] = dot(select_ref[i], rows[at + i]).astype(LOW)

        pl.when(step - experts < half)(lambda: put(keep_ref))
        pl.when(step - experts >= half)(lambda: put(send_ref))


def combine(lhs, weight, select, first, columns, transposed, sizes, flip):
    experts, pairs, count, units = lhs.shape
    blocks, tokens, slots = select.shape
    nx, ny, nz = sizes
    half = nx * ny
    at = first // columns

    def place(group):
        return group % ny * nx + group // ny if flip else group

    def keep_map(s):
        return (place(jnp.clip(s - experts, 0, half - 1)), 0, 0, 0)

    def send_map(s):
        return (place(jnp.clip(s - experts - half, 0, half - 1)), 0, 0, 0)

    if transposed:
        weight_spec = pl.BlockSpec(
            (1, pairs, columns, units), lambda s: (jnp.minimum(s, experts - 1), 0, at, 0)
        )
    else:
        weight_spec = pl.BlockSpec(
            (1, pairs, units, columns), lambda s: (jnp.minimum(s, experts - 1), 0, 0, at)
        )
    keep, send = pl.pallas_call(
        functools.partial(combine_kernel, transposed, experts),
        grid=(experts + 2 * half,),
        in_specs=[
            pl.BlockSpec(
                (1, pairs, count, units), lambda s: (jnp.minimum(s, experts - 1), 0, 0, 0)
            ),
            weight_spec,
            pl.BlockSpec((nz, tokens, slots), lambda s: (jnp.clip(s - experts, 0, 2 * half - 1), 0, 0)),
        ],
        out_specs=[
            pl.BlockSpec((1, nz, tokens, columns), keep_map),
            pl.BlockSpec((1, nz, tokens, columns), send_map),
        ],
        out_shape=[jax.ShapeDtypeStruct((half, nz, tokens, columns), LOW)] * 2,
        scratch_shapes=[pltpu.VMEM((blocks, slots, columns), LOW)],
        compiler_params=params(48),
        cost_estimate=cost(
            2 * lhs.size * columns + 2 * select.size * columns,
            2 * lhs.size + 2 * select.size + 4 * half * nz * tokens * columns,
        ),
        name="combine",
    )(lhs, weight, select)
    shape = (ny, nx, nz, tokens, columns) if flip else (nx, ny, nz, tokens, columns)
    return keep.reshape(shape), send.reshape(shape)


def weight_grad_kernel(left_ref, right_ref, out_ref):
    out_ref[0, 0] = dot(left_ref[0, 0], right_ref[0, 0], TN)


def weight_grad(left, right, tile_left, tile_right):
    experts, left_pairs, count, left_width = left.shape
    _, right_pairs, _, right_width = right.shape
    pairs = max(left_pairs, right_pairs)

    def left_map(e, i, j, p):
        return (e, p if left_pairs > 1 else 0, 0, i)

    def right_map(e, i, j, p):
        return (e, p if right_pairs > 1 else 0, 0, j)

    return pl.pallas_call(
        weight_grad_kernel,
        grid=(experts, left_width // tile_left, right_width // tile_right, pairs),
        in_specs=[
            pl.BlockSpec((1, 1, count, tile_left), left_map),
            pl.BlockSpec((1, 1, count, tile_right), right_map),
        ],
        out_specs=pl.BlockSpec((1, 1, tile_left, tile_right), lambda e, i, j, p: (e, p, i, j)),
        out_shape=jax.ShapeDtypeStruct((experts, pairs, left_width, right_width), WIDE),
        compiler_params=params(48),
        cost_estimate=cost(
            2 * experts * pairs * count * left_width * right_width,
            2 * left.size + 2 * right.size + 4 * experts * pairs * left_width * right_width,
        ),
        name="weight_grad",
    )(left, right)


def shards(
    hidden,
    segments,
    routes,
    attn_gain,
    qkv_weight,
    qk_gain,
    out_weight,
    moe_gain,
    router_weight,
    expert_up,
    expert_down,
    cotangent,
):
    tok_rows, width = hidden.shape
    length = segments.shape[0]
    head_width = out_weight.shape[0]
    local_heads = head_width // HEAD_DIM
    local_experts = expert_up.shape[0]
    all_experts = router_weight.shape[1]
    nz, ny, nx, ncore = (lax.axis_size(axis) for axis in ALL)
    n_tensor = nx * ncore
    blocks = nz * ny * n_tensor
    capacity = max(2, 3 * length // (16 * n_tensor))
    capacity = -(-capacity // 16) * 16
    slots = local_experts * capacity
    scale = HEAD_DIM ** (-0.5)
    expert_index = lax.axis_index("z") * ny + lax.axis_index("y")
    normed, inverse_attn = normalize(hidden, attn_gain)
    normed_all = lax.all_gather(normed.astype(LOW), TENSOR, axis=0, tiled=True)
    cotangent_all = lax.all_gather(cotangent.astype(LOW), ALL, axis=0, tiled=True)
    routes_all = lax.all_gather(routes, ALL, axis=0, tiled=True)

    order = block_order(("core", "x", "y", "z"))
    own_experts = expert_index * local_experts + jnp.arange(local_experts, dtype=jnp.int32)
    named = routes_all.reshape(blocks, tok_rows, -1)[order]
    member = jnp.any(named[:, None, :, :] == own_experts[None, :, None, None], axis=-1)
    token = jnp.arange(tok_rows, dtype=jnp.int32)
    earlier = (token[:, None] < token[None, :]).astype(LOW)
    rank = jnp.einsum("beu,ut->bet", member.astype(LOW), earlier, preferred_element_type=WIDE)
    rank = jnp.where(member, rank.astype(jnp.int32), -1)
    slot = jnp.arange(capacity, dtype=jnp.int32)
    chosen = rank[:, :, None, :] == slot[None, None, :, None]
    select = chosen.reshape(blocks, slots, tok_rows).astype(LOW)
    rank_back = jnp.swapaxes(rank, 1, 2)
    select_back = (rank_back[:, :, :, None] == slot).reshape(blocks, tok_rows, slots).astype(LOW)

    projected = jnp.einsum("td,cdf->tcf", normed_all, qkv_weight, preferred_element_type=WIDE)
    head_shape = (length, local_heads, HEAD_DIM)
    gains = qk_gain.reshape(2, local_heads, HEAD_DIM)
    cosine, sine = rope_tables(doc_positions(segments), HEAD_DIM // 2)
    query_pre = projected[:, 0].reshape(head_shape)
    key_pre = projected[:, 1].reshape(head_shape)
    query_normed, query_inverse = normalize(query_pre, gains[0])
    key_normed, key_inverse = normalize(key_pre, gains[1])
    queries = rotate(query_normed, cosine, sine).astype(LOW)
    keys_low = rotate(key_normed, cosine, sine).astype(LOW)
    values_low = projected[:, 2].reshape(head_shape).astype(LOW)
    index = jnp.arange(length, dtype=jnp.int32)
    allowed = ((segments[:, None] == segments[None, :]) & (index[:, None] >= index[None, :]))[None]

    def masked_scores():
        scores = jnp.einsum("qhd,khd->hqk", queries, keys_low, preferred_element_type=WIDE) * scale
        return jnp.where(allowed, scores, -1e30)

    masked = masked_scores()
    top = jnp.max(masked, axis=-1, keepdims=True)
    total = jnp.log(jnp.sum(jnp.exp(masked - top), axis=-1, keepdims=True)) + top
    weights_low = jnp.exp(masked - total).astype(LOW)
    mixed = jnp.einsum("hqk,khd->qhd", weights_low, values_low, preferred_element_type=WIDE)
    mixed = mixed.reshape(length, head_width).astype(LOW)

    def scatter_tensor(partial):
        parts = partial.reshape(nx, ncore, tok_rows, width)
        core = lax.axis_index("core")
        own = lax.dynamic_index_in_dim(parts, core, 1, keepdims=False)
        other = lax.dynamic_index_in_dim(parts, 1 - core, 1, keepdims=False)
        parts = add_low(own, swap(other, "core"))
        return line_scatter(parts, "x")

    attended = hidden + scatter_tensor(
        jnp.dot(mixed, out_weight, preferred_element_type=WIDE).astype(LOW)
    ).astype(WIDE)
    moe_normed, inverse_moe = normalize(attended, moe_gain)
    routed_low = moe_normed.astype(LOW)
    routed_all = lax.all_gather(routed_low, ALL, axis=0, tiled=True)
    logits = jnp.dot(routed_low, router_weight, preferred_element_type=WIDE)
    shifted = jnp.exp(logits - jnp.max(logits, axis=-1, keepdims=True))
    probs = shifted / jnp.sum(shifted, axis=-1, keepdims=True)
    probs_all = lax.all_gather(probs, ALL, axis=0, tiled=True)

    grad_slots = dispatch(order, select, cotangent_all, local_experts)
    grad_units = grad_active(grad_slots, expert_down)
    own_probs = lax.dynamic_slice_in_dim(
        probs_all.reshape(blocks, tok_rows, all_experts)[order],
        expert_index * local_experts,
        local_experts,
        axis=2,
    )
    slot_gates = jnp.sum(
        jnp.where(chosen, jnp.swapaxes(own_probs, 1, 2)[:, :, None, :], 0.0), axis=-1
    )
    slot_gates = jnp.swapaxes(slot_gates, 0, 1).reshape(local_experts, blocks * capacity, 1)
    row_slots = dispatch(order, select, routed_all, local_experts)
    gated_act, grad_pair, gate_grads = hidden_units(row_slots, expert_up, grad_units, slot_gates)

    gate_grads = jnp.swapaxes(gate_grads.reshape(local_experts, blocks, capacity), 0, 1)
    own_grads = jnp.sum(jnp.where(chosen, gate_grads[:, :, :, None], 0.0), axis=2)
    placed = lax.dynamic_update_slice_in_dim(
        jnp.zeros((blocks, tok_rows, all_experts), WIDE),
        jnp.swapaxes(own_grads, 1, 2),
        expert_index * local_experts,
        axis=2,
    ).reshape(ncore, nx, ny, nz, tok_rows, all_experts)
    grad_probs = scatter_all(placed[0], placed[1], ("x", "y", "z"))

    sizes = (nx, ny, nz)
    chunk = 512

    def sums(lhs, weight, transposed):
        pieces = []
        for first in range(0, width, chunk):
            flip = first // chunk % 2 == 1
            keep, send = combine(lhs, weight, select_back, first, chunk, transposed, sizes, flip)
            pieces.append(scatter_all(keep, send, ("y", "x", "z") if flip else ("x", "y", "z")))
        return jnp.concatenate(pieces, axis=-1).astype(WIDE)

    rows_back = sums(grad_pair, expert_up, True)
    outputs = sums(gated_act[:, None], expert_down[:, None], False)
    output = attended + outputs

    chose = jnp.any(routes[:, :, None] == jnp.arange(all_experts, dtype=jnp.int32), axis=1)
    grad_probs = jnp.where(chose, grad_probs, 0.0)
    grad_logits = probs * (grad_probs - jnp.sum(probs * grad_probs, axis=-1, keepdims=True))
    logits_low = grad_logits.astype(LOW)
    router_grad = jnp.einsum("td,te->de", routed_low, logits_low, preferred_element_type=WIDE)
    grad_moe = jnp.einsum("te,de->td", logits_low, router_weight, preferred_element_type=WIDE)
    grad_moe = grad_moe + rows_back
    grad_attended, moe_gain_grad = norm_back(grad_moe, attended, inverse_moe, moe_gain)
    grad_attended = grad_attended + cotangent
    piece = lax.all_gather(grad_attended.astype(LOW), TENSOR, axis=0, tiled=True)

    up_grad = weight_grad(row_slots[:, None], grad_pair, 512, expert_up.shape[-1])
    down_grad = weight_grad(gated_act[:, None], grad_slots[:, None], expert_up.shape[-1], 512)
    down_grad = down_grad.reshape(expert_down.shape)

    out_acc = jnp.einsum("tf,td->fd", mixed, piece, preferred_element_type=WIDE).astype(LOW)
    out_grad = sum_expert(out_acc)
    grad_mixed = jnp.einsum("td,fd->tf", piece, out_weight, preferred_element_type=WIDE).astype(LOW)
    grad_heads = grad_mixed.reshape(head_shape)
    recomputed = masked_scores()
    weights_wide = jnp.exp(recomputed - total)
    grad_weights = jnp.einsum("qhd,khd->hqk", grad_heads, values_low, preferred_element_type=WIDE)
    grad_scores = (
        weights_wide * (grad_weights - jnp.sum(grad_weights * weights_wide, axis=-1, keepdims=True))
    ).astype(LOW)
    grad_values = jnp.einsum("hqk,qhd->khd", weights_low, grad_heads, preferred_element_type=WIDE)
    grad_queries = jnp.einsum("hqk,khd->qhd", grad_scores, keys_low, preferred_element_type=WIDE)
    grad_keys = jnp.einsum("hqk,qhd->khd", grad_scores, queries, preferred_element_type=WIDE)
    grad_query_pre, query_gain_grad = norm_back(
        rotate(grad_queries * scale, cosine, -sine), query_pre, query_inverse, gains[0]
    )
    grad_key_pre, key_gain_grad = norm_back(
        rotate(grad_keys * scale, cosine, -sine), key_pre, key_inverse, gains[1]
    )
    grad_proj = [
        grad.reshape(length, head_width).astype(LOW)
        for grad in (grad_query_pre, grad_key_pre, grad_values)
    ]
    qk_gain_grad = jnp.stack([query_gain_grad.reshape(-1), key_gain_grad.reshape(-1)])
    grad_normed = sum(
        jnp.einsum("tf,df->td", grad, weight, preferred_element_type=WIDE)
        for grad, weight in zip(grad_proj, qkv_weight)
    ).astype(LOW)
    grad_normed = scatter_tensor(grad_normed).astype(WIDE)
    qkv_grad = jnp.stack(
        [
            sum_expert(
                jnp.einsum("td,tf->df", normed_all, grad, preferred_element_type=WIDE).astype(LOW)
            )
            for grad in grad_proj
        ]
    )
    grad_hidden, attn_gain_grad = norm_back(grad_normed, hidden, inverse_attn, attn_gain)
    grad_hidden = grad_hidden + grad_attended
    qk_gain_grad = lax.psum(qk_gain_grad, EXPERT)
    router_grad = lax.psum(router_grad, ALL)
    attn_gain_grad, moe_gain_grad = sum_all(jnp.stack([attn_gain_grad, moe_gain_grad]))
    return (
        output,
        grad_hidden,
        attn_gain_grad,
        qkv_grad,
        qk_gain_grad,
        out_grad,
        moe_gain_grad,
        router_grad,
        up_grad,
        down_grad,
    )


def solution(mesh):
    expert, tensor = (mesh.shape[name] for name in ("expert", "tensor"))
    grid = Mesh(mesh.devices.reshape(4, expert // 4, tensor // 2, 2), ALL)
    return jax.shard_map(
        shards,
        mesh=grid,
        in_specs=(
            P(ALL, None),
            P(EXPERT),
            P(ALL, None),
            P(),
            P(None, None, TENSOR),
            P(None, TENSOR),
            P(TENSOR, None),
            P(),
            P(),
            P(EXPERT, None, None, TENSOR),
            P(EXPERT, TENSOR, None),
            P(ALL, None),
        ),
        out_specs=(
            P(ALL, None),
            P(ALL, None),
            P(),
            P(None, None, TENSOR),
            P(None, TENSOR),
            P(TENSOR, None),
            P(),
            P(),
            P(EXPERT, None, None, TENSOR),
            P(EXPERT, TENSOR, None),
        ),
        check_vma=False,
    )
```

```python
import functools
import math

import jax
import jax.numpy as jnp
from jax import lax
from jax.experimental import pallas as pl
from jax.experimental.pallas import tpu as pltpu
from jax.sharding import Mesh, PartitionSpec as P

HEAD_DIM = 128
LOW = jnp.bfloat16
WIDE = jnp.float32


EPSILON = 1e-05
THETA = 10000.0


def normalize(values, gain):
    inverse = lax.rsqrt(jnp.mean(values * values, axis=-1, keepdims=True) + EPSILON)
    return (values * inverse * gain, inverse)


def norm_back(grad_out, values, inverse, gain):
    scaled = values * inverse
    weighted = grad_out * gain
    grad_in = inverse * (weighted - scaled * jnp.mean(weighted * scaled, axis=-1, keepdims=True))
    return (grad_in, jnp.sum(grad_out * scaled, axis=0))


def doc_starts(segment_ids):
    index = jnp.arange(segment_ids.shape[0], dtype=jnp.int32)
    starts = jnp.concatenate([jnp.ones((1,), jnp.bool_), segment_ids[1:] != segment_ids[:-1]])
    return lax.cummax(jnp.where(starts, index, 0), axis=0)


def rope_tables(positions, half):
    freq = jnp.exp(-math.log(THETA) * jnp.arange(half, dtype=jnp.float32) / half)
    angle = positions.astype(jnp.float32)[:, None] * freq[None, :]
    cosine, sine = jnp.cos(angle), jnp.sin(angle)
    return (
        jnp.concatenate([cosine, cosine], axis=-1),
        jnp.concatenate([-sine, sine], axis=-1),
    )


def add_low(*terms):
    total = terms[0].astype(WIDE)
    for term in terms[1:]:
        total = total + term.astype(WIDE)
    return total.astype(terms[0].dtype)


def tie(values, *before):
    return lax.optimization_barrier((values,) + before)[0]


class Grid:
    def __init__(self, expert, tensor):
        y_bits, x_bits = (expert // 4).bit_length() - 1, (tensor // 2).bit_length() - 1
        self.z = ("z1", "z0")
        self.y = tuple(f"y{i}" for i in reversed(range(y_bits)))
        self.x = tuple(f"x{i}" for i in reversed(range(x_bits)))
        self.core = ("core",)
        self.expert = self.z + self.y
        self.tensor = self.x + self.core
        self.all = self.expert + self.tensor


def swap(values, axis):
    return lax.ppermute(values, axis, [(0, 1), (1, 0)])


def pick(parts, index):
    return lax.dynamic_index_in_dim(parts, index, 0, keepdims=False)


def index_of(axes):
    index = jnp.int32(0)
    for axis in axes:
        index = index * 2 + lax.axis_index(axis)
    return index


def block_order(grid, axes):
    order = jnp.zeros((1,), jnp.int32)
    for axis in axes:
        stride = 1 << (len(grid.all) - 1 - grid.all.index(axis))
        own = lax.axis_index(axis)
        order = (order[:, None] + jnp.stack([own, 1 - own])[None, :] * stride).reshape(-1)
    return order


def halves(total):
    return total.reshape((2, total.shape[0] // 2) + total.shape[1:])


def scatter(total, axes):
    for axis in axes:
        parts = halves(total)
        total = add_low(parts[0], swap(parts[1], axis))
    return total


def scatter_rows(total, axes):
    for axis in axes:
        me = lax.axis_index(axis)
        parts = halves(total)
        total = add_low(pick(parts, me), swap(pick(parts, 1 - me), axis))
    return total


def gather_rows(values, axes):
    for axis in reversed(axes):
        me = lax.axis_index(axis)
        other = swap(values, axis)
        values = jnp.concatenate(
            [jnp.where(me == 0, values, other), jnp.where(me == 0, other, values)]
        )
    return values


def gather_relative(values, axes):
    for axis in axes:
        values = jnp.concatenate([values, swap(values, axis)])
    return values


def gather_tensor(values, grid):
    rows, width = values.shape
    pieces = gather_rows(gather_rows(values, grid.x), grid.core)
    return jnp.swapaxes(pieces.reshape(2, -1, rows, width), 0, 1).reshape(-1, width)


def scatter_tensor(partial, grid):
    rows, width = partial.shape
    parts = jnp.swapaxes(partial.reshape(1 << len(grid.x), 2, -1, width), 0, 1)
    return scatter_rows(parts.reshape(rows, width), grid.core + grid.x)


def sum_over(values, axes):
    for axis in axes:
        values = values + swap(values, axis)
    return values


def sum_expert(values, grid):
    axes = grid.y + grid.z[::-1]
    return gather_rows(scatter_rows(values, axes), axes).astype(WIDE)


NT = (((1,), (1,)), ((), ()))
TN = (((0,), (0,)), ((), ()))


def dot(left, right, dims=None):
    if dims is None:
        return jnp.dot(left, right, preferred_element_type=WIDE)
    return lax.dot_general(left, right, dims, preferred_element_type=WIDE)


def params(megabytes):
    return pltpu.CompilerParams(vmem_limit_bytes=megabytes << 20)


def cost(flops, moved):
    return pl.CostEstimate(flops=int(2 * flops), bytes_accessed=int(2 * moved), transcendentals=0)


def dispatch_kernel(order_ref, select_ref, rows_ref, out_ref):
    experts, capacity, width = out_ref.shape
    picked = dot(select_ref[0], rows_ref[0])
    out_ref[...] = picked.astype(LOW).reshape(experts, capacity, width)


def dispatch(order, select, rows, experts):
    blocks, slots, tokens = select.shape
    width = rows.shape[-1]
    capacity = slots // experts
    return pl.pallas_call(
        dispatch_kernel,
        grid_spec=pltpu.PrefetchScalarGridSpec(
            num_scalar_prefetch=1,
            grid=(blocks,),
            in_specs=[
                pl.BlockSpec((1, slots, tokens), lambda b, order: (b, 0, 0)),
                pl.BlockSpec((1, tokens, width), lambda b, order: (order[b], 0, 0)),
            ],
            out_specs=pl.BlockSpec((experts, capacity, width), lambda b, order: (0, b, 0)),
        ),
        out_shape=jax.ShapeDtypeStruct((experts, blocks * capacity, width), LOW),
        compiler_params=params(32),
        cost_estimate=cost(2 * blocks * slots * tokens * width, 2 * blocks * (slots + tokens) * width),
        name="dispatch",
    )(order, select, rows.reshape(blocks, tokens, width))


def row_tile(rows):
    return max(t for t in range(128, 513, 128) if rows % t == 0)


def grad_active_kernel(rows_ref, down_ref, out_ref):
    out_ref[0] = dot(rows_ref[0], down_ref[0], NT)


def grad_active(rows, expert_down):
    experts, count, width = rows.shape
    units = expert_down.shape[1]
    tile = row_tile(count)
    return pl.pallas_call(
        grad_active_kernel,
        grid=(experts, count // tile),
        in_specs=[
            pl.BlockSpec((1, tile, width), lambda e, r: (e, r, 0)),
            pl.BlockSpec((1, units, width), lambda e, r: (e, 0, 0)),
        ],
        out_specs=pl.BlockSpec((1, tile, units), lambda e, r: (e, r, 0)),
        out_shape=jax.ShapeDtypeStruct((experts, count, units), WIDE),
        compiler_params=params(32),
        cost_estimate=cost(2 * rows.size * units, 2 * rows.size),
        name="grad_active",
    )(rows, expert_down)


def hidden_kernel(rows_ref, up_ref, grad_ref, gate_ref, act_ref, pair_ref, gate_grad_ref):
    rows = rows_ref[0]
    gate_pre = dot(rows, up_ref[0, 0])
    upper = dot(rows, up_ref[0, 1])
    gate = gate_ref[0]
    sigma = jax.nn.sigmoid(gate_pre)
    silu = gate_pre * sigma
    active = silu * upper
    grad = grad_ref[0]
    gated = gate * grad
    act_ref[0] = (gate * active).astype(LOW)
    pair_ref[0, 0] = (gated * upper * (sigma * (1.0 + gate_pre * (1.0 - sigma)))).astype(LOW)
    pair_ref[0, 1] = (gated * silu).astype(LOW)
    gate_grad_ref[0] = jnp.sum(active * grad, axis=-1, keepdims=True)


def hidden_units(rows, expert_up, grads, gates):
    experts, count, width = rows.shape
    units = expert_up.shape[-1]
    tile = row_tile(count)
    return pl.pallas_call(
        hidden_kernel,
        grid=(experts, count // tile),
        in_specs=[
            pl.BlockSpec((1, tile, width), lambda e, r: (e, r, 0)),
            pl.BlockSpec((1, 2, width, units), lambda e, r: (e, 0, 0, 0)),
            pl.BlockSpec((1, tile, units), lambda e, r: (e, r, 0)),
            pl.BlockSpec((1, tile, 1), lambda e, r: (e, r, 0)),
        ],
        out_specs=[
            pl.BlockSpec((1, tile, units), lambda e, r: (e, r, 0)),
            pl.BlockSpec((1, 2, tile, units), lambda e, r: (e, 0, r, 0)),
            pl.BlockSpec((1, tile, 1), lambda e, r: (e, r, 0)),
        ],
        out_shape=[
            jax.ShapeDtypeStruct((experts, count, units), LOW),
            jax.ShapeDtypeStruct((experts, 2, count, units), LOW),
            jax.ShapeDtypeStruct((experts, count, 1), WIDE),
        ],
        compiler_params=params(40),
        cost_estimate=cost(4 * rows.size * units, 2 * rows.size),
        name="hidden_units",
    )(rows, expert_up, grads, gates)


def combine_kernel(transposed, experts, adds, group_of, *refs):
    lhs_ref, weight_ref, select_ref = refs[:3]
    received = refs[3] if adds else None
    outs, rows = refs[3 + adds : -1], refs[-1]
    step = pl.program_id(0)
    blocks, slots, columns = rows.shape
    capacity = slots // experts
    group = select_ref.shape[0]
    pairs = lhs_ref.shape[1]
    many = math.gcd(blocks, 8)

    @pl.when(step < experts)
    def _():
        start = pl.multiple_of(step * capacity, capacity)
        for first in range(0, blocks, many):
            piece = pl.ds(first * capacity, many * capacity)
            total = None
            for i in range(pairs):
                term = dot(lhs_ref[0, i, piece, :], weight_ref[0, i], NT if transposed else None)
                total = term if total is None else total + term
            rows[first : first + many, pl.ds(start, capacity), :] = total.astype(LOW).reshape(
                many, capacity, columns
            )

    @pl.when(step >= experts)
    def _():
        at = group_of(step) * group

        def put(ref):
            for i in range(group):
                total = dot(select_ref[i], rows[at + i])
                if adds:
                    total = total + received[0, i].astype(WIDE)
                ref[0, i] = total.astype(LOW)

        if adds:
            half = blocks // group // 2
            pl.when(step - experts < half)(lambda: put(outs[0]))
            pl.when(step - experts >= half)(lambda: put(outs[1]))
        else:
            put(outs[0])


def combine(lhs, weight, select, received, at, columns, transposed, sizes, flip, after=()):
    experts, pairs, count, units = lhs.shape
    blocks, tokens, slots = select.shape
    nx, ny, nz = sizes
    groups = nx * ny
    blocks //= 2
    count //= 2
    adds = received is not None
    part = 0 if adds else 1

    def group_of(s):
        place = jnp.clip(s - experts, 0, groups - 1)
        return place % nx * ny + place // nx if flip else place

    def expert_of(s):
        return jnp.minimum(s, experts - 1)

    if transposed:
        weight_spec = pl.BlockSpec((1, pairs, columns, units), lambda s: (expert_of(s), 0, at, 0))
    else:
        weight_spec = pl.BlockSpec((1, pairs, units, columns), lambda s: (expert_of(s), 0, 0, at))
    in_specs = [
        pl.BlockSpec((1, pairs, count, units), lambda s: (expert_of(s), 0, part, 0)),
        weight_spec,
        pl.BlockSpec((nz, tokens, slots), lambda s: (part * groups + group_of(s), 0, 0)),
    ]
    operands = [lhs, weight, select]
    if adds:
        in_specs.append(
            pl.BlockSpec((1, nz, tokens, columns), lambda s: (jnp.clip(s - experts, 0, groups - 1), 0, 0, 0))
        )
        operands.append(received)
        half = groups // 2
        out_specs = [
            pl.BlockSpec(
                (1, nz, tokens, columns), lambda s: (jnp.clip(s - experts, 0, half - 1), 0, 0, 0)
            ),
            pl.BlockSpec(
                (1, nz, tokens, columns), lambda s: (jnp.clip(s - experts - half, 0, half - 1), 0, 0, 0)
            ),
        ]
        out_shape = [jax.ShapeDtypeStruct((half, nz, tokens, columns), LOW)] * 2
    else:
        out_specs = [
            pl.BlockSpec(
                (1, nz, tokens, columns), lambda s: (jnp.clip(s - experts, 0, groups - 1), 0, 0, 0)
            )
        ]
        out_shape = [jax.ShapeDtypeStruct((groups, nz, tokens, columns), LOW)]
    return pl.pallas_call(
        without(len(operands), len(after), functools.partial(combine_kernel, transposed, experts, adds, group_of)),
        grid=(experts + groups,),
        in_specs=in_specs + [pl.BlockSpec(memory_space=pl.ANY)] * len(after),
        out_specs=out_specs,
        out_shape=out_shape,
        scratch_shapes=[pltpu.VMEM((blocks, slots, columns), LOW)],
        compiler_params=params(48),
        cost_estimate=cost(
            2 * lhs.size * columns + 2 * select.size * columns,
            2 * lhs.size + 2 * select.size + (12 if adds else 4) * blocks * tokens * columns,
        ),
        name="combine_own" if adds else "combine_other",
    )(*operands, *after)


def without(first, count, kernel):
    def run(*refs):
        kernel(*refs[:first], *refs[first + count :])

    return run


def spread(rows, columns, width):
    return (
        lax.broadcasted_iota(jnp.int32, (rows, width), 0),
        lax.broadcasted_iota(jnp.int32, (rows, width), 1) + columns,
    )


def turn(values, cosine, sine):
    return values * cosine + pltpu.roll(values, HEAD_DIM // 2, 1) * sine


def mean_last(values):
    return jnp.mean(values, axis=-1, keepdims=True)


def attention_kernel(tile, pre_ref, gain_ref, cos_ref, sin_ref, first_ref, out_refs, mixed_ref, lse_ref):
    length = pre_ref.shape[1]
    cosine, sine = cos_ref[...], sin_ref[...]
    for i in range(2):
        pre = pre_ref[i]
        inverse = lax.rsqrt(mean_last(pre * pre) + EPSILON)
        out_refs[i] = turn(pre * inverse * gain_ref[i], cosine, sine).astype(LOW)
    values = pre_ref[2].astype(LOW)
    out_refs[2] = values
    values_turned = values.T
    for start in range(0, length, tile):
        end = start + tile
        block = pl.ds(start, tile)
        scores = dot(out_refs[1, :end], out_refs[0, block], NT) * HEAD_DIM ** (-0.5)
        key, query = spread(end, start, tile)
        allowed = (key <= query) & (key >= first_ref[:, block])
        scores = jnp.where(allowed, scores, -1e30)
        top = jnp.max(scores, axis=0, keepdims=True)
        weights = jnp.exp(scores - top)
        total = jnp.sum(weights, axis=0, keepdims=True)
        lse_ref[0, :, block] = jnp.log(total) + top
        weights = (weights * (1.0 / total)).astype(LOW)
        mixed_ref[block, :] = dot(values_turned[:, :end], weights).T.astype(LOW)


def attention(projected, gains, cosine, sine, first):
    _, length, width = projected.shape
    tile = math.gcd(length, 256)
    head = lambda h: (0, 0, h)
    whole = lambda h: (0, 0)
    return pl.pallas_call(
        functools.partial(attention_kernel, tile),
        grid=(width // HEAD_DIM,),
        in_specs=[
            pl.BlockSpec((3, length, HEAD_DIM), head),
            pl.BlockSpec((2, 1, HEAD_DIM), head),
            pl.BlockSpec((length, HEAD_DIM), whole),
            pl.BlockSpec((length, HEAD_DIM), whole),
            pl.BlockSpec((1, length), whole),
        ],
        out_specs=[
            pl.BlockSpec((3, length, HEAD_DIM), head),
            pl.BlockSpec((length, HEAD_DIM), lambda h: (0, h)),
            pl.BlockSpec((1, 1, length), lambda h: (h, 0, 0)),
        ],
        out_shape=[
            jax.ShapeDtypeStruct(projected.shape, LOW),
            jax.ShapeDtypeStruct((length, width), LOW),
            jax.ShapeDtypeStruct((width // HEAD_DIM, 1, length), WIDE),
        ],
        compiler_params=params(48),
        cost_estimate=cost(6 * length * length * width, 40 * length * width),
        name="attention",
    )(projected, gains[:, None, :], cosine, sine, first)


def attention_back_kernel(
    tile,
    pre_ref,
    gain_ref,
    cos_ref,
    sin_ref,
    first_ref,
    low_ref,
    lse_ref,
    grad_ref,
    out_refs,
    gain_grad_ref,
    query_grad,
    key_grad,
    value_grad,
):
    length = pre_ref.shape[1]
    scale = HEAD_DIM ** (-0.5)
    keys_turned = low_ref[1].T
    for start in reversed(range(0, length, tile)):
        end = start + tile
        block = pl.ds(start, tile)
        queries, grads = low_ref[0, block], grad_ref[block, :]
        scores = dot(low_ref[1, :end], queries, NT) * scale
        key, query = spread(end, start, tile)
        allowed = (key <= query) & (key >= first_ref[:, block])
        weights = jnp.where(allowed, jnp.exp(scores - lse_ref[0, :, block]), 0.0)
        grad_weights = dot(low_ref[2, :end], grads, NT)
        mean = jnp.sum(grad_weights * weights, axis=0, keepdims=True)
        grad_scores = (weights * (grad_weights - mean)).astype(LOW)
        query_grad[block, :] = dot(keys_turned[:, :end], grad_scores).T
        key_term = dot(grad_scores, queries)
        value_term = dot(weights.astype(LOW), grads)
        if end == length:
            key_grad[...] = key_term
            value_grad[...] = value_term
        else:
            key_grad[:end] += key_term
            value_grad[:end] += value_term
    out_refs[2] = value_grad[...].astype(LOW)
    cosine, sine = cos_ref[...], sin_ref[...]
    for i, grad in enumerate((query_grad, key_grad)):
        grad = turn(grad[...] * scale, cosine, -sine)
        pre = pre_ref[i]
        inverse = lax.rsqrt(mean_last(pre * pre) + EPSILON)
        scaled = pre * inverse
        weighted = grad * gain_ref[i]
        out_refs[i] = (inverse * (weighted - scaled * mean_last(weighted * scaled))).astype(LOW)
        gain_grad_ref[i] = jnp.sum(grad * scaled, axis=0, keepdims=True)


def attention_back(projected, gains, cosine, sine, first, low, lse, grads, after=()):
    _, length, width = projected.shape
    tile = math.gcd(length, 256)
    head = lambda h: (0, 0, h)
    whole = lambda h: (0, 0)
    return pl.pallas_call(
        without(8, len(after), functools.partial(attention_back_kernel, tile)),
        grid=(width // HEAD_DIM,),
        in_specs=[
            pl.BlockSpec((3, length, HEAD_DIM), head),
            pl.BlockSpec((2, 1, HEAD_DIM), head),
            pl.BlockSpec((length, HEAD_DIM), whole),
            pl.BlockSpec((length, HEAD_DIM), whole),
            pl.BlockSpec((1, length), whole),
            pl.BlockSpec((3, length, HEAD_DIM), head),
            pl.BlockSpec((1, 1, length), lambda h: (h, 0, 0)),
            pl.BlockSpec((length, HEAD_DIM), lambda h: (0, h)),
        ]
        + [pl.BlockSpec(memory_space=pl.ANY)] * len(after),
        out_specs=[
            pl.BlockSpec((3, length, HEAD_DIM), head),
            pl.BlockSpec((2, 1, HEAD_DIM), head),
        ],
        out_shape=[
            jax.ShapeDtypeStruct(projected.shape, LOW),
            jax.ShapeDtypeStruct((2, 1, width), WIDE),
        ],
        scratch_shapes=[pltpu.VMEM((length, HEAD_DIM), WIDE)] * 3,
        compiler_params=params(48),
        cost_estimate=cost(14 * length * length * width, 40 * length * width),
        name="attention_back",
    )(projected, gains[:, None, :], cosine, sine, first, low, lse, grads, *after)


def weight_grad_kernel(left_ref, right_ref, out_ref):
    out_ref[0, 0] = dot(left_ref[0, 0], right_ref[0, 0], TN)


def weight_grad(left, right, tile_left, tile_right, first, last, into=None, after=()):
    experts, left_pairs, count, left_width = left.shape
    _, right_pairs, _, right_width = right.shape
    pairs = max(left_pairs, right_pairs)

    def left_map(e, i, j, p):
        return (e + first, p if left_pairs > 1 else 0, 0, i)

    def right_map(e, i, j, p):
        return (e + first, p if right_pairs > 1 else 0, 0, j)

    rest = ([] if into is None else [into]) + list(after)
    return pl.pallas_call(
        without(2, len(rest), weight_grad_kernel),
        grid=(last - first, left_width // tile_left, right_width // tile_right, pairs),
        in_specs=[
            pl.BlockSpec((1, 1, count, tile_left), left_map),
            pl.BlockSpec((1, 1, count, tile_right), right_map),
        ]
        + [pl.BlockSpec(memory_space=pl.ANY)] * len(rest),
        out_specs=pl.BlockSpec(
            (1, 1, tile_left, tile_right), lambda e, i, j, p: (e + first, p, i, j)
        ),
        out_shape=jax.ShapeDtypeStruct((experts, pairs, left_width, right_width), WIDE),
        input_output_aliases={} if into is None else {2: 0},
        compiler_params=params(48),
        cost_estimate=cost(
            2 * (last - first) * pairs * count * left_width * right_width,
            (2 * left.size + 2 * right.size + 4 * experts * pairs * left_width * right_width)
            * (last - first)
            // experts,
        ),
        name="weight_grad",
    )(left, right, *rest)


def shards(
    grid,
    hidden,
    segments,
    routes,
    attn_gain,
    qkv_weight,
    qk_gain,
    out_weight,
    moe_gain,
    router_weight,
    expert_up,
    expert_down,
    cotangent,
):
    tok_rows, width = hidden.shape
    length = segments.shape[0]
    local_experts = expert_up.shape[0]
    all_experts = router_weight.shape[1]
    nz, ny, nx = (1 << len(axes) for axes in (grid.z, grid.y, grid.x))
    n_tensor = nx * 2
    blocks = nz * ny * n_tensor
    capacity = max(2, 3 * length // (16 * n_tensor))
    capacity = -(-capacity // 16) * 16
    slots = local_experts * capacity
    expert_index = index_of(grid.expert)
    order_x = grid.x[::-1] + grid.y[::-1] + grid.z[::-1]
    order_y = grid.y[::-1] + grid.x[::-1] + grid.z[::-1]
    normed, inverse_attn = normalize(hidden, attn_gain)
    normed_all = gather_tensor(normed.astype(LOW), grid)
    cotangent_all = lax.all_gather(cotangent.astype(LOW), grid.all, axis=0, tiled=True)
    named = gather_relative(routes.T[None], (grid.core + order_x)[::-1])

    order = block_order(grid, grid.core + order_x)
    own_experts = expert_index * local_experts + jnp.arange(local_experts, dtype=jnp.int32)
    member = jnp.any(named[:, None, :, :] == own_experts[None, :, None, None], axis=2)
    token = jnp.arange(tok_rows, dtype=jnp.int32)
    earlier = (token[:, None] < token[None, :]).astype(LOW)
    rank = jnp.einsum("beu,ut->bet", member.astype(LOW), earlier, preferred_element_type=WIDE)
    rank = jnp.where(member, rank.astype(jnp.int32), -1)
    slot = jnp.arange(capacity, dtype=jnp.int32)
    chosen = rank[:, :, None, :] == slot[None, None, :, None]
    select = chosen.reshape(blocks, slots, tok_rows).astype(LOW)
    rank_back = jnp.swapaxes(rank, 1, 2)
    select_back = (rank_back[:, :, :, None] == slot).reshape(blocks, tok_rows, slots).astype(LOW)

    projected = jnp.einsum("td,cdf->ctf", normed_all, qkv_weight, preferred_element_type=WIDE)
    first_key = doc_starts(segments)
    cosine, sine = rope_tables(jnp.arange(length, dtype=jnp.int32) - first_key, HEAD_DIM // 2)
    first_key = first_key[None]
    heads_low, mixed, lse = attention(projected, qk_gain, cosine, sine, first_key)
    attended = hidden + scatter_tensor(
        jnp.dot(mixed, out_weight, preferred_element_type=WIDE).astype(LOW), grid
    ).astype(WIDE)
    moe_normed, inverse_moe = normalize(attended, moe_gain)
    routed_low = moe_normed.astype(LOW)
    routed_low, cotangent_all = lax.optimization_barrier((routed_low, cotangent_all))
    routed_all = lax.all_gather(routed_low, grid.all, axis=0, tiled=True)
    logits = jnp.dot(routed_low, router_weight, preferred_element_type=WIDE)
    shifted = jnp.exp(logits - jnp.max(logits, axis=-1, keepdims=True))
    probs = shifted / jnp.sum(shifted, axis=-1, keepdims=True)
    own_probs = probs.T[None]
    for axis in (grid.core + order_x)[::-1]:
        if axis in grid.expert:
            me = lax.axis_index(axis)
            count, columns, tokens = own_probs.shape
            parts = jnp.swapaxes(own_probs.reshape(count, 2, columns // 2, tokens), 0, 1)
            own_probs = jnp.concatenate(
                [pick(parts, me), swap(pick(parts, 1 - me), axis)]
            )
        else:
            own_probs = jnp.concatenate([own_probs, swap(own_probs, axis)])

    grad_slots = dispatch(order, select, cotangent_all, local_experts)
    grad_units = grad_active(grad_slots, expert_down)
    slot_gates = jnp.sum(
        jnp.where(chosen, own_probs[:, :, None, :], 0.0), axis=-1
    )
    slot_gates = jnp.swapaxes(slot_gates, 0, 1).reshape(local_experts, blocks * capacity, 1)
    row_slots = dispatch(order, select, routed_all, local_experts)
    gated_act, grad_pair, gate_grads = hidden_units(row_slots, expert_up, grad_units, slot_gates)

    gate_grads = jnp.swapaxes(gate_grads.reshape(local_experts, blocks, capacity), 0, 1)
    own_grads = jnp.sum(jnp.where(chosen, gate_grads[:, :, :, None], 0.0), axis=2)
    sizes = (nx, ny, nz)
    chunk = 512
    act, down_weight = gated_act[:, None], expert_down[:, None]
    units = expert_up.shape[-1]

    def to_other(lhs, weight, transposed, at, flip, after):
        (other,) = combine(
            lhs, weight, select_back, None, at, chunk, transposed, sizes, flip, after
        )
        return other, swap(other, "core")

    def to_own(lhs, weight, transposed, at, flip, received, after):
        return combine(
            lhs, weight, select_back, received, at, chunk, transposed, sizes, flip, after
        )

    def step(total, axis):
        parts = halves(total)
        return add_low(parts[0], swap(parts[1], axis))

    def first(own, rest, axis):
        total = add_low(own, swap(rest, axis))
        return total.reshape((-1,) + total.shape[2:])

    def gather_experts(values, axis):
        parts = halves(values)
        other = swap(parts[1], axis)
        me = lax.axis_index(axis)
        return jnp.concatenate(
            [jnp.where(me == 0, parts[0], other), jnp.where(me == 0, other, parts[0])], axis=1
        )

    orders = (order_x, order_y, order_x, order_y)
    grads = (grad_pair, expert_up, True)
    outs = (act, down_weight, False)
    other, sent, own, total = [None] * 4, [None] * 4, [None] * 4, [None] * 4
    small = own_grads
    small_steps = [functools.partial(lambda axis, v: step(v, axis), axis) for axis in grid.core + grid.x[::-1]]
    small_steps += [
        functools.partial(lambda axis, v: gather_experts(v, axis), axis) for axis in order_x[len(grid.x) :]
    ]
    before = ()
    for name, i in (
        ("other", 0),
        ("other", 1),
        ("own", 0),
        ("own", 1),
        ("other", 2),
        ("other", 3),
        ("own", 2),
    ):
        if name == "other":
            other[i], sent[i] = to_other(*grads, i, i % 2 == 1, before)
            before = (other[i],)
        else:
            own[i] = to_own(*grads, i, i % 2 == 1, sent[i], before)
            before = (own[i][0],)
        if small_steps:
            small = small_steps.pop(0)(tie(small, before[0]))
            before += (small,)
    for run in small_steps:
        small = run(small)
    grad_probs = small[0].T
    for i in (0, 1):
        total[i] = first(*own[i], orders[i][0])
    own[3] = to_own(*grads, 3, True, sent[3], before + (total[0], total[1]))
    o_other, o_sent, o_own = [None] * 4, [None] * 4, [None] * 4
    o_other[0], o_sent[0] = to_other(*outs, 0, False, (own[3][0],))
    for i in (0, 1):
        total[i] = step(total[i], orders[i][1])
    o_other[1], o_sent[1] = to_other(*outs, 1, False, (o_other[0], total[0], total[1]))
    o_own[0] = to_own(*outs, 0, False, o_sent[0], (o_other[1],))
    for i in (0, 1):
        total[i] = step(total[i], orders[i][2])
    for i in (2, 3):
        total[i] = first(*own[i], orders[i][0])
    o_other[2], o_sent[2] = to_other(*outs, 2, False, (o_own[0][0],) + tuple(total))
    o_own[1] = to_own(*outs, 1, False, o_sent[1], (o_other[2],))
    for i in (0, 1):
        total[i] = step(total[i], orders[i][3])
    for i in (2, 3):
        total[i] = step(total[i], orders[i][1])
    o_other[3], o_sent[3] = to_other(*outs, 3, False, (o_own[1][0],) + tuple(total))
    for i in (2, 3):
        total[i] = step(total[i], orders[i][2])
    o_own[2] = to_own(*outs, 2, False, o_sent[2], (o_other[3], total[2], total[3]))
    for i in (2, 3):
        total[i] = step(total[i], orders[i][3])
    for i in range(4):
        total[i] = scatter(total[i], orders[i][4:])[0]
    rows_back = jnp.concatenate(total, axis=-1).astype(WIDE)

    chose = jnp.any(routes[:, :, None] == jnp.arange(all_experts, dtype=jnp.int32), axis=1)
    grad_probs = jnp.where(chose, grad_probs, 0.0)
    grad_logits = probs * (grad_probs - jnp.sum(probs * grad_probs, axis=-1, keepdims=True))
    logits_low = grad_logits.astype(LOW)
    router_grad = jnp.einsum("td,te->de", routed_low, logits_low, preferred_element_type=WIDE)
    grad_moe = jnp.einsum("te,de->td", logits_low, router_weight, preferred_element_type=WIDE)
    grad_moe = grad_moe + rows_back
    grad_attended, moe_gain_grad = norm_back(grad_moe, attended, inverse_moe, moe_gain)
    grad_attended = grad_attended + cotangent
    grad_low = grad_attended.astype(LOW)
    piece = gather_tensor(grad_low, grid)

    o_own[3] = to_own(*outs, 3, False, o_sent[3], (grad_low, o_own[2][0]))
    piece = tie(piece, o_own[3][0])
    outputs = []
    for i in range(4):
        mine, rest = o_own[i]
        outputs.append(scatter(first(mine, tie(rest, piece), order_x[0]), order_x[1:])[0])
    output = attended + jnp.concatenate(outputs, axis=-1).astype(WIDE)

    grad_mixed = jnp.einsum("td,fd->tf", piece, out_weight, preferred_element_type=WIDE).astype(LOW)
    out_acc = jnp.einsum(
        "tf,td->fd", mixed, tie(piece, grad_mixed), preferred_element_type=WIDE
    ).astype(LOW)
    out_grad = sum_expert(out_acc, grid)
    grad_proj, qk_gain_grad = attention_back(
        projected, qk_gain, cosine, sine, first_key, heads_low, lse, grad_mixed, (out_acc,)
    )
    qk_gain_grad = qk_gain_grad.reshape(2, -1)
    grad_normed = jnp.einsum(
        "ctf,cdf->td", grad_proj, qkv_weight, preferred_element_type=WIDE
    ).astype(LOW)
    qkv_parts = [
        jnp.einsum("td,tf->df", normed_all, grad_proj[i], preferred_element_type=WIDE).astype(LOW)
        for i in range(3)
    ]
    down_grad = weight_grad(
        act, grad_slots[:, None], units, 512, 0, local_experts, None, tuple(qkv_parts) + (grad_normed,)
    )
    up_grad = weight_grad(
        row_slots[:, None], grad_pair, 512, units, 0, local_experts, None, (down_grad,)
    )
    down_grad = down_grad.reshape(expert_down.shape)
    qkv_grad = jnp.stack([sum_expert(part, grid) for part in qkv_parts])
    grad_normed = scatter_tensor(grad_normed, grid).astype(WIDE)
    grad_hidden, attn_gain_grad = norm_back(grad_normed, hidden, inverse_attn, attn_gain)
    grad_hidden = grad_hidden + grad_attended
    qk_gain_grad = sum_over(qk_gain_grad, grid.expert)
    router_grad = lax.psum(router_grad, grid.all)
    attn_gain_grad, moe_gain_grad = sum_over(
        jnp.stack([attn_gain_grad, moe_gain_grad]), grid.all[::-1]
    )
    return (
        output,
        grad_hidden,
        attn_gain_grad,
        qkv_grad,
        qk_gain_grad,
        out_grad,
        moe_gain_grad,
        router_grad,
        up_grad,
        down_grad,
    )


def solution(mesh):
    grid = Grid(mesh.shape["expert"], mesh.shape["tensor"])
    devices = Mesh(mesh.devices.reshape((2,) * len(grid.all)), grid.all)
    rows = P(grid.all, None)
    return jax.shard_map(
        functools.partial(shards, grid),
        mesh=devices,
        in_specs=(
            rows,
            P(grid.expert),
            rows,
            P(),
            P(None, None, grid.tensor),
            P(None, grid.tensor),
            P(grid.tensor, None),
            P(),
            P(),
            P(grid.expert, None, None, grid.tensor),
            P(grid.expert, grid.tensor, None),
            rows,
        ),
        out_specs=(
            rows,
            rows,
            P(),
            P(None, None, grid.tensor),
            P(None, grid.tensor),
            P(grid.tensor, None),
            P(),
            P(),
            P(grid.expert, None, None, grid.tensor),
            P(grid.expert, grid.tensor, None),
        ),
        check_vma=False,
    )
```

```python
import functools
import math

import jax
import jax.numpy as jnp
from jax import lax
from jax.experimental import pallas as pl
from jax.experimental.pallas import tpu as pltpu
from jax.sharding import Mesh, PartitionSpec as P

HEAD_DIM = 128
LOW = jnp.bfloat16
WIDE = jnp.float32
EST = 100


EPSILON = 1e-05
THETA = 10000.0


def normalize(values, gain):
    inverse = lax.rsqrt(jnp.mean(values * values, axis=-1, keepdims=True) + EPSILON)
    return (values * inverse * gain, inverse)


def norm_back(grad_out, values, inverse, gain):
    scaled = values * inverse
    weighted = grad_out * gain
    grad_in = inverse * (weighted - scaled * jnp.mean(weighted * scaled, axis=-1, keepdims=True))
    return (grad_in, jnp.sum(grad_out * scaled, axis=0))


def doc_starts(segment_ids):
    index = jnp.arange(segment_ids.shape[0], dtype=jnp.int32)
    starts = jnp.concatenate([jnp.ones((1,), jnp.bool_), segment_ids[1:] != segment_ids[:-1]])
    return lax.cummax(jnp.where(starts, index, 0), axis=0)


def rope_tables(positions, half):
    freq = jnp.exp(-math.log(THETA) * jnp.arange(half, dtype=jnp.float32) / half)
    angle = positions.astype(jnp.float32)[:, None] * freq[None, :]
    cosine, sine = jnp.cos(angle), jnp.sin(angle)
    return (
        jnp.concatenate([cosine, cosine], axis=-1),
        jnp.concatenate([-sine, sine], axis=-1),
    )


def add_low(*terms):
    total = terms[0].astype(WIDE)
    for term in terms[1:]:
        total = total + term.astype(WIDE)
    return total.astype(terms[0].dtype)


def tie(values, *before):
    return lax.optimization_barrier((values,) + before)[0]


class Grid:
    def __init__(self, expert, tensor):
        y_bits, x_bits = (expert // 4).bit_length() - 1, (tensor // 2).bit_length() - 1
        self.z = ("z1", "z0")
        self.y = tuple(f"y{i}" for i in reversed(range(y_bits)))
        self.x = tuple(f"x{i}" for i in reversed(range(x_bits)))
        self.core = ("core",)
        self.expert = self.z + self.y
        self.tensor = self.x + self.core
        self.all = self.expert + self.tensor


def swap(values, axis):
    return lax.ppermute(values, axis, [(0, 1), (1, 0)])


def pick(parts, index):
    return lax.dynamic_index_in_dim(parts, index, 0, keepdims=False)


def index_of(axes):
    index = jnp.int32(0)
    for axis in axes:
        index = index * 2 + lax.axis_index(axis)
    return index


def block_order(grid, axes):
    order = jnp.zeros((1,), jnp.int32)
    for axis in axes:
        stride = 1 << (len(grid.all) - 1 - grid.all.index(axis))
        own = lax.axis_index(axis)
        order = (order[:, None] + jnp.stack([own, 1 - own])[None, :] * stride).reshape(-1)
    return order


def halves(total):
    return total.reshape((2, total.shape[0] // 2) + total.shape[1:])


class Transfers:
    def __init__(self, steps, zero=None):
        self.steps = steps
        self.result = None
        self.sent, axis = next(steps)
        if zero is not None:
            self.sent = later(self.sent, zero)
        self.moving = swap(self.sent, axis)

    def advance(self, zero=None):
        if self.result is not None:
            return
        try:
            arrived = self.moving if zero is None else later(self.moving, zero)
            self.sent, axis = self.steps.send(arrived)
            self.moving = swap(self.sent, axis)
        except StopIteration as stop:
            self.sent = self.result = stop.value

    def finish(self):
        while self.result is None:
            self.advance()
        return self.result


def later(values, done):
    return values + done[0, 0].astype(values.dtype)


def advance(transfers, done):
    sent = [done]
    for one in transfers:
        one.advance(done)
        sent.append(one.sent)
    return tuple(sent)


def scattering(own, rest, axes):
    total = add_low(own, (yield rest, axes[0]))
    total = total.reshape((-1,) + total.shape[2:])
    for axis in axes[1:]:
        parts = halves(total)
        total = add_low(parts[0], (yield parts[1], axis))
    return total[0]


def scattering_rows(total, axes):
    for axis in axes:
        me = lax.axis_index(axis)
        parts = halves(total)
        total = add_low(pick(parts, me), (yield pick(parts, 1 - me), axis))
    return total


def gathering_rows(values, axes):
    for axis in reversed(axes):
        me = lax.axis_index(axis)
        other = yield values, axis
        values = jnp.concatenate(
            [jnp.where(me == 0, values, other), jnp.where(me == 0, other, values)]
        )
    return values


def summing(values, axes):
    own = yield from scattering_rows(values, axes)
    return (yield from gathering_rows(own, axes))


def scattering_tensor(partial, grid):
    rows, width = partial.shape
    parts = jnp.swapaxes(partial.reshape(1 << len(grid.x), 2, -1, width), 0, 1)
    return (yield from scattering_rows(parts.reshape(rows, width), grid.core + grid.x))


def gather_relative(values, axes):
    for axis in axes:
        values = jnp.concatenate([values, swap(values, axis)])
    return values


def gather_tensor(values, grid):
    rows, width = values.shape
    pieces = Transfers(gathering_rows(values, grid.core + grid.x)).finish()
    return jnp.swapaxes(pieces.reshape(2, -1, rows, width), 0, 1).reshape(-1, width)


def pair_steps(values, axes):
    for axis in axes:
        values = values + (yield values, axis)
    return values


NT = (((1,), (1,)), ((), ()))
TN = (((0,), (0,)), ((), ()))


def dot(left, right, dims=None):
    if dims is None:
        return jnp.dot(left, right, preferred_element_type=WIDE)
    return lax.dot_general(left, right, dims, preferred_element_type=WIDE)


def params(megabytes):
    return pltpu.CompilerParams(vmem_limit_bytes=megabytes << 20)


def cost(flops, moved):
    return pl.CostEstimate(flops=int(flops / EST), bytes_accessed=int(moved / EST), transcendentals=0)


def dispatch_kernel(order_ref, select_ref, rows_ref, out_ref):
    experts, capacity, width = out_ref.shape
    picked = dot(select_ref[0], rows_ref[0])
    out_ref[...] = picked.astype(LOW).reshape(experts, capacity, width)


def dispatch(order, select, rows, experts):
    blocks, slots, tokens = select.shape
    width = rows.shape[-1]
    capacity = slots // experts
    return pl.pallas_call(
        dispatch_kernel,
        grid_spec=pltpu.PrefetchScalarGridSpec(
            num_scalar_prefetch=1,
            grid=(blocks,),
            in_specs=[
                pl.BlockSpec((1, slots, tokens), lambda b, order: (b, 0, 0)),
                pl.BlockSpec((1, tokens, width), lambda b, order: (order[b], 0, 0)),
            ],
            out_specs=pl.BlockSpec((experts, capacity, width), lambda b, order: (0, b, 0)),
        ),
        out_shape=jax.ShapeDtypeStruct((experts, blocks * capacity, width), LOW),
        compiler_params=params(32),
        cost_estimate=cost(2 * blocks * slots * tokens * width, 2 * blocks * (slots + tokens) * width),
        name="dispatch",
    )(order, select, rows.reshape(blocks, tokens, width))


def row_tile(rows):
    return max(t for t in range(128, 513, 128) if rows % t == 0)


def grad_active_kernel(rows_ref, down_ref, out_ref):
    out_ref[0] = dot(rows_ref[0], down_ref[0], NT)


def grad_active(rows, expert_down):
    experts, count, width = rows.shape
    units = expert_down.shape[1]
    tile = row_tile(count)
    return pl.pallas_call(
        grad_active_kernel,
        grid=(experts, count // tile),
        in_specs=[
            pl.BlockSpec((1, tile, width), lambda e, r: (e, r, 0)),
            pl.BlockSpec((1, units, width), lambda e, r: (e, 0, 0)),
        ],
        out_specs=pl.BlockSpec((1, tile, units), lambda e, r: (e, r, 0)),
        out_shape=jax.ShapeDtypeStruct((experts, count, units), WIDE),
        compiler_params=params(32),
        cost_estimate=cost(2 * rows.size * units, 2 * rows.size),
        name="grad_active",
    )(rows, expert_down)


def hidden_kernel(rows_ref, up_ref, grad_ref, gate_ref, act_ref, pair_ref, gate_grad_ref):
    rows = rows_ref[0]
    gate_pre = dot(rows, up_ref[0, 0])
    upper = dot(rows, up_ref[0, 1])
    tile = rows.shape[0]
    gate = jnp.broadcast_to(gate_ref[0], (128, tile)).T[:, :1]
    sigma = jax.nn.sigmoid(gate_pre)
    silu = gate_pre * sigma
    active = silu * upper
    grad = grad_ref[0]
    gated = gate * grad
    act_ref[0] = (gate * active).astype(LOW)
    pair_ref[0, 0] = (gated * upper * (sigma * (1.0 + gate_pre * (1.0 - sigma)))).astype(LOW)
    pair_ref[0, 1] = (gated * silu).astype(LOW)
    gate_grad = jnp.sum(active * grad, axis=-1, keepdims=True)
    gate_grad_ref[0] = jnp.broadcast_to(gate_grad, (tile, 128)).T[:1]


def hidden_units(rows, expert_up, grads, gates):
    experts, count, width = rows.shape
    units = expert_up.shape[-1]
    tile = row_tile(count)
    return pl.pallas_call(
        hidden_kernel,
        grid=(experts, count // tile),
        in_specs=[
            pl.BlockSpec((1, tile, width), lambda e, r: (e, r, 0)),
            pl.BlockSpec((1, 2, width, units), lambda e, r: (e, 0, 0, 0)),
            pl.BlockSpec((1, tile, units), lambda e, r: (e, r, 0)),
            pl.BlockSpec((1, 1, tile), lambda e, r: (e, 0, r)),
        ],
        out_specs=[
            pl.BlockSpec((1, tile, units), lambda e, r: (e, r, 0)),
            pl.BlockSpec((1, 2, tile, units), lambda e, r: (e, 0, r, 0)),
            pl.BlockSpec((1, 1, tile), lambda e, r: (e, 0, r)),
        ],
        out_shape=[
            jax.ShapeDtypeStruct((experts, count, units), LOW),
            jax.ShapeDtypeStruct((experts, 2, count, units), LOW),
            jax.ShapeDtypeStruct((experts, 1, count), WIDE),
        ],
        compiler_params=params(40),
        cost_estimate=cost(4 * rows.size * units, 2 * rows.size),
        name="hidden_units",
    )(rows, expert_up, grads, gates)


def combine_kernel(transposed, experts, adds, extra, group_of, groups, *refs):
    lhs_ref, weight_ref, select_ref = refs[:3]
    refs = refs[3:]
    if extra:
        gate_ref, first_ref, refs = refs[0], refs[1], refs[2:]
    received, refs = (refs[:groups], refs[groups:]) if adds else ((None,) * groups, refs)
    outs, done_ref, rows = refs[:-2], refs[-2], refs[-1]
    step = pl.program_id(0)
    done_ref[...] = jnp.zeros_like(done_ref)
    blocks, slots, columns = rows.shape
    capacity = slots // experts
    group = select_ref.shape[0]
    pairs = lhs_ref.shape[1]
    many = math.gcd(blocks, 8)

    @pl.when(step < experts)
    def _():
        start = pl.multiple_of(step * capacity, capacity)
        for first in range(0, blocks, many):
            piece = pl.ds(first * capacity, many * capacity)
            total = None
            for i in range(pairs):
                term = dot(lhs_ref[0, i, piece, :], weight_ref[0, i], NT if transposed else None)
                total = term if total is None else total + term
            shape = (many, capacity, total.shape[-1])
            if extra:
                gates = jnp.broadcast_to(gate_ref[0, :, piece], (128, many * capacity)).T
                lane = lax.broadcasted_iota(jnp.int32, gates.shape, 1)
                gates = jnp.where(lane == first_ref[0] + step, gates, 0.0)
                rows[first : first + many, pl.ds(start, capacity), shape[-1] :] = gates.astype(
                    LOW
                ).reshape(many, capacity, 128)
            rows[first : first + many, pl.ds(start, capacity), : shape[-1]] = total.astype(
                LOW
            ).reshape(shape)

    @pl.when(step >= experts)
    def _():
        at = group_of(step) * group

        def put(out, more):
            for i in range(group):
                total = dot(select_ref[i], rows[at + i])
                if adds:
                    total = total + more[0, i].astype(WIDE)
                out[0, i] = total.astype(LOW)

        each = groups // len(outs)
        for place in range(groups):
            pl.when(step - experts == place)(
                functools.partial(put, outs[place // each], received[place])
            )


def combine(lhs, weight, select, received, at, columns, transposed, sizes, flip, after=(), gates=None):
    experts, pairs, count, units = lhs.shape
    blocks, tokens, slots = select.shape
    nx, ny, nz = sizes
    groups = nx * ny
    blocks //= 2
    count //= 2
    adds = received is not None
    part = 0 if adds else 1

    def group_of(s):
        place = jnp.clip(s - experts, 0, groups - 1)
        return place % nx * ny + place // nx if flip else place

    def expert_of(s):
        return jnp.minimum(s, experts - 1)

    if transposed:
        weight_spec = pl.BlockSpec((1, pairs, columns, units), lambda s: (expert_of(s), 0, at, 0))
    else:
        weight_spec = pl.BlockSpec((1, pairs, units, columns), lambda s: (expert_of(s), 0, 0, at))
    in_specs = [
        pl.BlockSpec((1, pairs, count, units), lambda s: (expert_of(s), 0, part, 0)),
        weight_spec,
        pl.BlockSpec((nz, tokens, slots), lambda s: (part * groups + group_of(s), 0, 0)),
    ]
    operands = [lhs, weight, select]
    if gates is not None:
        in_specs += [
            pl.BlockSpec((1, 1, count), lambda s: (expert_of(s), 0, part)),
            pl.BlockSpec(memory_space=pltpu.SMEM),
        ]
        operands += gates
        columns += 128
    if adds:
        in_specs += [pl.BlockSpec((1, nz, tokens, columns), lambda s: (0, 0, 0, 0))] * groups
        operands += received
        outs, half = 2, groups // 2
        place_of = lambda o, s: jnp.clip(s - experts - o * half, 0, half - 1)
    else:
        outs, half = groups, 1
        place_of = lambda o, s: 0
    out_specs = [
        pl.BlockSpec((1, nz, tokens, columns), functools.partial(lambda o, s: (place_of(o, s), 0, 0, 0), o))
        for o in range(outs)
    ]
    kernel = functools.partial(
        combine_kernel, transposed, experts, adds, gates is not None, group_of, groups
    )
    return pl.pallas_call(
        without(len(operands), len(after), kernel),
        grid=(experts + groups,),
        in_specs=in_specs + [pl.BlockSpec(memory_space=pl.ANY)] * len(after),
        out_specs=out_specs + [pl.BlockSpec((8, 128), lambda s: (0, 0))],
        out_shape=[jax.ShapeDtypeStruct((half, nz, tokens, columns), LOW)] * outs
        + [jax.ShapeDtypeStruct((8, 128), WIDE)],
        scratch_shapes=[pltpu.VMEM((blocks, slots, columns), LOW)],
        compiler_params=params(56),
        cost_estimate=cost(
            2 * lhs.size * columns + 2 * select.size * columns,
            2 * lhs.size + 2 * select.size + (12 if adds else 4) * blocks * tokens * columns,
        ),
        name="combine_own" if adds else "combine_other",
    )(*operands, *after)


def without(first, count, kernel):
    def run(*refs):
        kernel(*refs[:first], *refs[first + count :])

    return run


def spread(rows, columns, width):
    return (
        lax.broadcasted_iota(jnp.int32, (rows, width), 0),
        lax.broadcasted_iota(jnp.int32, (rows, width), 1) + columns,
    )


def turn(values, cosine, sine):
    return values * cosine + pltpu.roll(values, HEAD_DIM // 2, 1) * sine


def mean_last(values):
    return jnp.mean(values, axis=-1, keepdims=True)


def attention_kernel(tile, pre_ref, gain_ref, cos_ref, sin_ref, first_ref, out_refs, mixed_ref, lse_ref):
    length = pre_ref.shape[1]
    cosine, sine = cos_ref[...], sin_ref[...]
    for i in range(2):
        pre = pre_ref[i]
        inverse = lax.rsqrt(mean_last(pre * pre) + EPSILON)
        out_refs[i] = turn(pre * inverse * gain_ref[i], cosine, sine).astype(LOW)
    values = pre_ref[2].astype(LOW)
    out_refs[2] = values
    values_turned = values.T
    for start in range(0, length, tile):
        end = start + tile
        block = pl.ds(start, tile)
        scores = dot(out_refs[1, :end], out_refs[0, block], NT) * HEAD_DIM ** (-0.5)
        key, query = spread(end, start, tile)
        allowed = (key <= query) & (key >= first_ref[:, block])
        scores = jnp.where(allowed, scores, -1e30)
        top = jnp.max(scores, axis=0, keepdims=True)
        weights = jnp.exp(scores - top)
        total = jnp.sum(weights, axis=0, keepdims=True)
        lse_ref[0, :, block] = jnp.log(total) + top
        weights = (weights * (1.0 / total)).astype(LOW)
        mixed_ref[block, :] = dot(values_turned[:, :end], weights).T.astype(LOW)


def attention(projected, gains, cosine, sine, first):
    _, length, width = projected.shape
    tile = math.gcd(length, 256)
    head = lambda h: (0, 0, h)
    whole = lambda h: (0, 0)
    return pl.pallas_call(
        functools.partial(attention_kernel, tile),
        grid=(width // HEAD_DIM,),
        in_specs=[
            pl.BlockSpec((3, length, HEAD_DIM), head),
            pl.BlockSpec((2, 1, HEAD_DIM), head),
            pl.BlockSpec((length, HEAD_DIM), whole),
            pl.BlockSpec((length, HEAD_DIM), whole),
            pl.BlockSpec((1, length), whole),
        ],
        out_specs=[
            pl.BlockSpec((3, length, HEAD_DIM), head),
            pl.BlockSpec((length, HEAD_DIM), lambda h: (0, h)),
            pl.BlockSpec((1, 1, length), lambda h: (h, 0, 0)),
        ],
        out_shape=[
            jax.ShapeDtypeStruct(projected.shape, LOW),
            jax.ShapeDtypeStruct((length, width), LOW),
            jax.ShapeDtypeStruct((width // HEAD_DIM, 1, length), WIDE),
        ],
        compiler_params=params(48),
        cost_estimate=cost(6 * length * length * width, 40 * length * width),
        name="attention",
    )(projected, gains[:, None, :], cosine, sine, first)


def attention_back_kernel(
    tile,
    pre_ref,
    gain_ref,
    cos_ref,
    sin_ref,
    first_ref,
    low_ref,
    lse_ref,
    grad_ref,
    out_refs,
    gain_grad_ref,
    done_ref,
    query_grad,
    key_grad,
    value_grad,
):
    length = pre_ref.shape[1]
    scale = HEAD_DIM ** (-0.5)
    done_ref[...] = jnp.zeros_like(done_ref)
    keys_turned = low_ref[1].T
    for start in reversed(range(0, length, tile)):
        end = start + tile
        block = pl.ds(start, tile)
        queries, grads = low_ref[0, block], grad_ref[block, :]
        scores = dot(low_ref[1, :end], queries, NT) * scale
        key, query = spread(end, start, tile)
        allowed = (key <= query) & (key >= first_ref[:, block])
        weights = jnp.where(allowed, jnp.exp(scores - lse_ref[0, :, block]), 0.0)
        grad_weights = dot(low_ref[2, :end], grads, NT)
        mean = jnp.sum(grad_weights * weights, axis=0, keepdims=True)
        grad_scores = (weights * (grad_weights - mean)).astype(LOW)
        query_grad[block, :] = dot(keys_turned[:, :end], grad_scores).T
        key_term = dot(grad_scores, queries)
        value_term = dot(weights.astype(LOW), grads)
        if end == length:
            key_grad[...] = key_term
            value_grad[...] = value_term
        else:
            key_grad[:end] += key_term
            value_grad[:end] += value_term
    out_refs[2] = value_grad[...].astype(LOW)
    cosine, sine = cos_ref[...], sin_ref[...]
    for i, grad in enumerate((query_grad, key_grad)):
        grad = turn(grad[...] * scale, cosine, -sine)
        pre = pre_ref[i]
        inverse = lax.rsqrt(mean_last(pre * pre) + EPSILON)
        scaled = pre * inverse
        weighted = grad * gain_ref[i]
        out_refs[i] = (inverse * (weighted - scaled * mean_last(weighted * scaled))).astype(LOW)
        gain_grad_ref[i] = jnp.sum(grad * scaled, axis=0, keepdims=True)


def attention_back(projected, gains, cosine, sine, first, low, lse, grads, after=()):
    _, length, width = projected.shape
    tile = math.gcd(length, 256)
    head = lambda h: (0, 0, h)
    whole = lambda h: (0, 0)
    return pl.pallas_call(
        without(8, len(after), functools.partial(attention_back_kernel, tile)),
        grid=(width // HEAD_DIM,),
        in_specs=[
            pl.BlockSpec((3, length, HEAD_DIM), head),
            pl.BlockSpec((2, 1, HEAD_DIM), head),
            pl.BlockSpec((length, HEAD_DIM), whole),
            pl.BlockSpec((length, HEAD_DIM), whole),
            pl.BlockSpec((1, length), whole),
            pl.BlockSpec((3, length, HEAD_DIM), head),
            pl.BlockSpec((1, 1, length), lambda h: (h, 0, 0)),
            pl.BlockSpec((length, HEAD_DIM), lambda h: (0, h)),
        ]
        + [pl.BlockSpec(memory_space=pl.ANY)] * len(after),
        out_specs=[
            pl.BlockSpec((3, length, HEAD_DIM), head),
            pl.BlockSpec((2, 1, HEAD_DIM), head),
            pl.BlockSpec((8, 128), whole),
        ],
        out_shape=[
            jax.ShapeDtypeStruct(projected.shape, LOW),
            jax.ShapeDtypeStruct((2, 1, width), WIDE),
            jax.ShapeDtypeStruct((8, 128), WIDE),
        ],
        scratch_shapes=[pltpu.VMEM((length, HEAD_DIM), WIDE)] * 3,
        compiler_params=params(48),
        cost_estimate=cost(14 * length * length * width, 40 * length * width),
        name="attention_back",
    )(projected, gains[:, None, :], cosine, sine, first, low, lse, grads, *after)


def weight_grad_kernel(left_ref, right_ref, out_ref, done_ref):
    out_ref[0, 0] = dot(left_ref[0, 0], right_ref[0, 0], TN)
    done_ref[...] = jnp.zeros_like(done_ref)


def weight_grad(left, right, tile_left, tile_right, first, last, into=None, after=()):
    experts, left_pairs, count, left_width = left.shape
    _, right_pairs, _, right_width = right.shape
    pairs = max(left_pairs, right_pairs)

    def left_map(e, i, j, p):
        return (e + first, p if left_pairs > 1 else 0, 0, i)

    def right_map(e, i, j, p):
        return (e + first, p if right_pairs > 1 else 0, 0, j)

    rest = ([] if into is None else [into]) + list(after)
    return pl.pallas_call(
        without(2, len(rest), weight_grad_kernel),
        grid=(last - first, left_width // tile_left, right_width // tile_right, pairs),
        in_specs=[
            pl.BlockSpec((1, 1, count, tile_left), left_map),
            pl.BlockSpec((1, 1, count, tile_right), right_map),
        ]
        + [pl.BlockSpec(memory_space=pl.ANY)] * len(rest),
        out_specs=[
            pl.BlockSpec((1, 1, tile_left, tile_right), lambda e, i, j, p: (e + first, p, i, j)),
            pl.BlockSpec((8, 128), lambda e, i, j, p: (0, 0)),
        ],
        out_shape=[
            jax.ShapeDtypeStruct((experts, pairs, left_width, right_width), WIDE),
            jax.ShapeDtypeStruct((8, 128), WIDE),
        ],
        input_output_aliases={} if into is None else {2: 0},
        compiler_params=params(48),
        cost_estimate=cost(
            2 * (last - first) * pairs * count * left_width * right_width,
            (2 * left.size + 2 * right.size + 4 * experts * pairs * left_width * right_width)
            * (last - first)
            // experts,
        ),
        name="weight_grad",
    )(left, right, *rest)


def shards(
    grid,
    hidden,
    segments,
    routes,
    attn_gain,
    qkv_weight,
    qk_gain,
    out_weight,
    moe_gain,
    router_weight,
    expert_up,
    expert_down,
    cotangent,
):
    tok_rows, width = hidden.shape
    length = segments.shape[0]
    local_experts = expert_up.shape[0]
    all_experts = router_weight.shape[1]
    nz, ny, nx = (1 << len(axes) for axes in (grid.z, grid.y, grid.x))
    n_tensor = nx * 2
    blocks = nz * ny * n_tensor
    capacity = max(2, 3 * length // (16 * n_tensor))
    capacity = -(-capacity // 16) * 16
    slots = local_experts * capacity
    expert_index = index_of(grid.expert)
    order_x = grid.x[::-1] + grid.y[::-1] + grid.z[::-1]
    order_y = grid.y[::-1] + grid.x[::-1] + grid.z[::-1]
    normed, inverse_attn = normalize(hidden, attn_gain)
    normed_all = gather_tensor(normed.astype(LOW), grid)
    cotangent_all = lax.all_gather(cotangent.astype(LOW), grid.all, axis=0, tiled=True)
    named = gather_relative(routes.T[None], (grid.core + order_x)[::-1])

    order = block_order(grid, grid.core + order_x)
    own_experts = expert_index * local_experts + jnp.arange(local_experts, dtype=jnp.int32)
    member = jnp.any(named[:, None, :, :] == own_experts[None, :, None, None], axis=2)
    token = jnp.arange(tok_rows, dtype=jnp.int32)
    earlier = (token[:, None] < token[None, :]).astype(LOW)
    rank = jnp.einsum("beu,ut->bet", member.astype(LOW), earlier, preferred_element_type=WIDE)
    rank = jnp.where(member, rank.astype(jnp.int32), -1)
    slot = jnp.arange(capacity, dtype=jnp.int32)
    chosen = rank[:, :, None, :] == slot[None, None, :, None]
    select = chosen.reshape(blocks, slots, tok_rows).astype(LOW)
    rank_back = jnp.swapaxes(rank, 1, 2)
    select_back = (rank_back[:, :, :, None] == slot).reshape(blocks, tok_rows, slots).astype(LOW)

    projected = jnp.einsum("td,cdf->ctf", normed_all, qkv_weight, preferred_element_type=WIDE)
    first_key = doc_starts(segments)
    cosine, sine = rope_tables(jnp.arange(length, dtype=jnp.int32) - first_key, HEAD_DIM // 2)
    first_key = first_key[None]
    heads_low, mixed, lse = attention(projected, qk_gain, cosine, sine, first_key)
    partial = jnp.dot(mixed, out_weight, preferred_element_type=WIDE).astype(LOW)
    attended = hidden + Transfers(scattering_tensor(partial, grid)).finish().astype(WIDE)
    moe_normed, inverse_moe = normalize(attended, moe_gain)
    routed_low = moe_normed.astype(LOW)
    routed_low, cotangent_all = lax.optimization_barrier((routed_low, cotangent_all))
    routed_all = lax.all_gather(routed_low, grid.all, axis=0, tiled=True)
    logits = jnp.dot(routed_low, router_weight, preferred_element_type=WIDE)
    shifted = jnp.exp(logits - jnp.max(logits, axis=-1, keepdims=True))
    probs = shifted / jnp.sum(shifted, axis=-1, keepdims=True)
    own_probs = probs.T[None]
    for axis in (grid.core + order_x)[::-1]:
        if axis in grid.expert:
            me = lax.axis_index(axis)
            count, columns, tokens = own_probs.shape
            parts = jnp.swapaxes(own_probs.reshape(count, 2, columns // 2, tokens), 0, 1)
            own_probs = jnp.concatenate(
                [pick(parts, me), swap(pick(parts, 1 - me), axis)]
            )
        else:
            own_probs = jnp.concatenate([own_probs, swap(own_probs, axis)])

    grad_slots = dispatch(order, select, cotangent_all, local_experts)
    grad_units = grad_active(grad_slots, expert_down)
    slot_gates = jnp.sum(
        jnp.where(chosen, own_probs[:, :, None, :], 0.0), axis=-1
    )
    slot_gates = jnp.swapaxes(slot_gates, 0, 1).reshape(local_experts, 1, blocks * capacity)
    row_slots = dispatch(order, select, routed_all, local_experts)
    gated_act, grad_pair, gate_grads = hidden_units(row_slots, expert_up, grad_units, slot_gates)

    sizes = (nx, ny, nz)
    chunk = 512
    act, down_weight = gated_act[:, None], expert_down[:, None]
    units = expert_up.shape[-1]

    def to_other(lhs, weight, transposed, at, flip, after, gates=None):
        parts = combine(
            lhs, weight, select_back, None, at, chunk, transposed, sizes, flip, after, gates
        )
        return parts[-1], [swap(part, "core") for part in parts[:-1]]

    def to_own(lhs, weight, transposed, at, flip, received, after, gates=None):
        return combine(
            lhs, weight, select_back, received, at, chunk, transposed, sizes, flip, after, gates
        )

    orders = (order_x, order_y, order_x, order_y)
    grads = (grad_pair, expert_up, True)
    outs = (act, down_weight, False)
    extra = [[gate_grads, (expert_index * local_experts)[None]], None, None, None]
    other, sent, own, rows = [None] * 4, [None] * 4, [None] * 4, [None] * 4

    def grad_other(i, before):
        done, sent[i] = to_other(*grads, i, i % 2 == 1, before, extra[i])
        return done

    def grad_own(i, before):
        *own, done = to_own(*grads, i, i % 2 == 1, sent[i], before, extra[i])
        rows[i] = Transfers(scattering(*own, orders[i]))
        return done

    o_sent, o_own, outputs = [None] * 4, [None] * 4, [None] * 4
    o_orders = (order_x, order_y, order_x, order_x)

    def out_other(i, before):
        done, o_sent[i] = to_other(*outs, i, i == 1, before)
        return done

    def out_own(i, before):
        *o_own[i], done = to_own(*outs, i, i == 1, o_sent[i], before)
        return done

    def out_start(i, done):
        outputs[i] = Transfers(scattering(*o_own[i], o_orders[i]), done)

    done = grad_other(0, ())
    done = grad_other(1, (done,))
    done = grad_own(0, (done,))
    done = grad_own(1, (done,))
    done = grad_other(2, (done,))
    done = grad_other(3, (done,))
    now = advance([rows[0]], done)
    done = grad_own(2, now)
    now = advance([rows[1]], done)
    done = grad_own(3, now)
    now = advance([rows[0]], done)
    done = out_other(0, now)
    done = out_other(1, (done,))
    now = advance([rows[0], rows[2]], done)
    done = out_own(0, now)
    now = advance([rows[1], rows[3], rows[0]], done)
    done = out_own(1, now)
    out_start(0, done)
    out_start(1, done)
    now = advance([rows[2], rows[1]], done)
    done = out_other(2, now)
    now = advance([rows[3], rows[1], rows[2]], done)
    done = out_other(3, now)
    advance([rows[2], rows[3]], done)
    advance([rows[3]], done)
    rows_back = jnp.concatenate([run.finish()[:, :chunk] for run in rows], axis=-1).astype(WIDE)
    grad_probs = rows[0].result[:, chunk : chunk + all_experts].astype(WIDE)

    chose = jnp.any(routes[:, :, None] == jnp.arange(all_experts, dtype=jnp.int32), axis=1)
    grad_probs = jnp.where(chose, grad_probs, 0.0)
    grad_logits = probs * (grad_probs - jnp.sum(probs * grad_probs, axis=-1, keepdims=True))
    logits_low = grad_logits.astype(LOW)
    router_grad = jnp.einsum("td,te->de", routed_low, logits_low, preferred_element_type=WIDE)
    grad_moe = jnp.einsum("te,de->td", logits_low, router_weight, preferred_element_type=WIDE)
    grad_moe = grad_moe + rows_back
    grad_attended, moe_gain_grad = norm_back(grad_moe, attended, inverse_moe, moe_gain)
    grad_attended = grad_attended + cotangent
    grad_low = grad_attended.astype(LOW)
    piece = gather_tensor(grad_low, grid)

    done = out_own(2, (grad_low,))
    done = out_own(3, (done,))
    now = advance([outputs[0], outputs[1]], done)
    piece = later(piece, done)
    out_start(2, done)
    out_start(3, done)

    sum_axes = grid.y + grid.z[::-1]
    grad_mixed = jnp.einsum("td,fd->tf", piece, out_weight, preferred_element_type=WIDE).astype(LOW)
    out_acc = jnp.einsum("tf,td->fd", mixed, piece, preferred_element_type=WIDE).astype(LOW)
    out_sum = Transfers(summing(out_acc, sum_axes))
    grad_proj, qk_gain_grad, done = attention_back(
        projected, qk_gain, cosine, sine, first_key, heads_low, lse, grad_mixed, (out_acc,) + now
    )
    qkv_sums = [
        Transfers(
            summing(
                jnp.einsum(
                    "td,tf->df", normed_all, grad_proj[i], preferred_element_type=WIDE
                ).astype(LOW),
                sum_axes,
            )
        )
        for i in (2, 0, 1)
    ]
    grad_normed = jnp.einsum(
        "ctf,cdf->td", grad_proj, qkv_weight, preferred_element_type=WIDE
    ).astype(LOW)
    normed_sum = Transfers(scattering_tensor(grad_normed, grid))
    gain_sum = Transfers(pair_steps(qk_gain_grad.reshape(2, -1), grid.expert))
    v_sum, q_sum, k_sum = qkv_sums
    now = (done, grad_normed) + tuple(run.sent for run in qkv_sums)
    gains = None
    waves = (
        (2, 0, [normed_sum, outputs[0], outputs[1], out_sum, v_sum]),
        (2, 0, [out_sum, v_sum, outputs[0], outputs[1], q_sum, k_sum, outputs[2]]),
        (2, 0, [normed_sum, out_sum, v_sum, q_sum, k_sum, outputs[0], outputs[1], gain_sum]),
        (2, 0, [out_sum, v_sum, q_sum, k_sum, outputs[3], outputs[2]]),
        (0, 4, [out_sum, v_sum, q_sum, k_sum, outputs[2], outputs[3], gain_sum]),
        (0, 4, [q_sum, k_sum, outputs[2], outputs[3]]),
        (0, 0, [outputs[3], gain_sum]),
    )

    def attention_norm_back(done):
        grad_normed = normed_sum.finish().astype(WIDE)
        grad_in, attn_gain_grad = norm_back(grad_normed, hidden, inverse_attn, attn_gain)
        both = jnp.stack([attn_gain_grad, moe_gain_grad])
        return grad_in + grad_attended, Transfers(pair_steps(both, grid.all[::-1]), done)

    up_left, down_left = list(range(local_experts)), list(range(local_experts))
    down_grad = up_grad = None
    for up_count, down_count, wave in waves:
        now_up, up_left = up_left[:up_count], up_left[up_count:]
        now_down, down_left = down_left[:down_count], down_left[down_count:]
        for e in now_up:
            up_grad, done = weight_grad(
                row_slots[:, None], grad_pair, 512, units, e, e + 1, up_grad, now
            )
            now = (done,)
        for e in now_down:
            down_grad, done = weight_grad(
                act, grad_slots[:, None], units, 512, e, e + 1, down_grad, now
            )
            now = (done,)
        now = advance(wave, done)
        if normed_sum.result is not None and gains is None:
            grad_hidden, gains = attention_norm_back(done)
        elif gains is not None:
            gains.advance(done)
    if gains is None:
        grad_hidden, gains = attention_norm_back(done)
    down_grad = down_grad.reshape(expert_down.shape)
    qkv_grad = jnp.stack([run.finish().astype(WIDE) for run in (q_sum, k_sum, v_sum)])
    out_grad = out_sum.finish().astype(WIDE)
    qk_gain_grad = gain_sum.finish()
    output = attended + jnp.concatenate([run.finish() for run in outputs], axis=-1).astype(WIDE)
    router_grad = lax.psum(router_grad, grid.all)
    attn_gain_grad, moe_gain_grad = gains.finish()
    return (
        output,
        grad_hidden,
        attn_gain_grad,
        qkv_grad,
        qk_gain_grad,
        out_grad,
        moe_gain_grad,
        router_grad,
        up_grad,
        down_grad,
    )


def solution(mesh):
    grid = Grid(mesh.shape["expert"], mesh.shape["tensor"])
    devices = Mesh(mesh.devices.reshape((2,) * len(grid.all)), grid.all)
    rows = P(grid.all, None)
    return jax.shard_map(
        functools.partial(shards, grid),
        mesh=devices,
        in_specs=(
            rows,
            P(grid.expert),
            rows,
            P(),
            P(None, None, grid.tensor),
            P(None, grid.tensor),
            P(grid.tensor, None),
            P(),
            P(),
            P(grid.expert, None, None, grid.tensor),
            P(grid.expert, grid.tensor, None),
            rows,
        ),
        out_specs=(
            rows,
            rows,
            P(),
            P(None, None, grid.tensor),
            P(None, grid.tensor),
            P(grid.tensor, None),
            P(),
            P(),
            P(grid.expert, None, None, grid.tensor),
            P(grid.expert, grid.tensor, None),
        ),
        check_vma=False,
    )
```

```python
import functools
import math

import jax
import jax.numpy as jnp
from jax import lax
from jax.experimental import pallas as pl
from jax.experimental.pallas import tpu as pltpu
from jax.sharding import Mesh, PartitionSpec as P

HEAD_DIM = 128
LOW = jnp.bfloat16
WIDE = jnp.float32
EST = 100


EPSILON = 1e-05
THETA = 10000.0


def normalize(values, gain):
    inverse = lax.rsqrt(jnp.mean(values * values, axis=-1, keepdims=True) + EPSILON)
    return (values * inverse * gain, inverse)


def norm_back(grad_out, values, inverse, gain):
    scaled = values * inverse
    weighted = grad_out * gain
    grad_in = inverse * (weighted - scaled * jnp.mean(weighted * scaled, axis=-1, keepdims=True))
    return (grad_in, jnp.sum(grad_out * scaled, axis=0))


def doc_starts(segment_ids):
    index = jnp.arange(segment_ids.shape[0], dtype=jnp.int32)
    starts = jnp.concatenate([jnp.ones((1,), jnp.bool_), segment_ids[1:] != segment_ids[:-1]])
    return lax.cummax(jnp.where(starts, index, 0), axis=0)


def rope_tables(positions, half):
    freq = jnp.exp(-math.log(THETA) * jnp.arange(half, dtype=jnp.float32) / half)
    angle = positions.astype(jnp.float32)[:, None] * freq[None, :]
    cosine, sine = jnp.cos(angle), jnp.sin(angle)
    return (
        jnp.concatenate([cosine, cosine], axis=-1),
        jnp.concatenate([-sine, sine], axis=-1),
    )


def add_low(*terms):
    total = terms[0].astype(WIDE)
    for term in terms[1:]:
        total = total + term.astype(WIDE)
    return total.astype(terms[0].dtype)


def tie(values, *before):
    return lax.optimization_barrier((values,) + before)[0]


class Grid:
    def __init__(self, expert, tensor):
        y_bits, x_bits = (expert // 4).bit_length() - 1, (tensor // 2).bit_length() - 1
        self.z = ("z1", "z0")
        self.y = tuple(f"y{i}" for i in reversed(range(y_bits)))
        self.x = tuple(f"x{i}" for i in reversed(range(x_bits)))
        self.core = ("core",)
        self.expert = self.z + self.y
        self.tensor = self.x + self.core
        self.all = self.expert + self.tensor


def swap(values, axis):
    return lax.ppermute(values, axis, [(0, 1), (1, 0)])


def pick(parts, index):
    return lax.dynamic_index_in_dim(parts, index, 0, keepdims=False)


def index_of(axes):
    index = jnp.int32(0)
    for axis in axes:
        index = index * 2 + lax.axis_index(axis)
    return index


def block_order(grid, axes):
    order = jnp.zeros((1,), jnp.int32)
    for axis in axes:
        stride = 1 << (len(grid.all) - 1 - grid.all.index(axis))
        own = lax.axis_index(axis)
        order = (order[:, None] + jnp.stack([own, 1 - own])[None, :] * stride).reshape(-1)
    return order


def halves(total):
    return total.reshape((2, total.shape[0] // 2) + total.shape[1:])


class Transfers:
    def __init__(self, steps, zero=None):
        self.steps = steps
        self.result = None
        self.sent, axis = next(steps)
        if zero is not None:
            self.sent = later(self.sent, zero)
        self.moving = swap(self.sent, axis)

    def advance(self, zero=None):
        if self.result is not None:
            return
        try:
            arrived = self.moving if zero is None else later(self.moving, zero)
            self.sent, axis = self.steps.send(arrived)
            self.moving = swap(self.sent, axis)
        except StopIteration as stop:
            self.sent = self.result = stop.value

    def finish(self):
        while self.result is None:
            self.advance()
        return self.result


def later(values, done):
    return values + done[0, 0].astype(values.dtype)


def advance(transfers, done):
    sent = [done]
    for one in transfers:
        one.advance(done)
        sent.append(one.sent)
    return tuple(sent)


def scattering(own, rest, axes):
    total = add_low(own, (yield rest, axes[0]))
    total = total.reshape((-1,) + total.shape[2:])
    for axis in axes[1:]:
        parts = halves(total)
        total = add_low(parts[0], (yield parts[1], axis))
    return total[0]


def scattering_rows(total, axes):
    for axis in axes:
        me = lax.axis_index(axis)
        parts = halves(total)
        total = add_low(pick(parts, me), (yield pick(parts, 1 - me), axis))
    return total


def gathering_rows(values, axes):
    for axis in reversed(axes):
        me = lax.axis_index(axis)
        other = yield values, axis
        values = jnp.concatenate(
            [jnp.where(me == 0, values, other), jnp.where(me == 0, other, values)]
        )
    return values


def summing(values, axes):
    own = yield from scattering_rows(values, axes)
    return (yield from gathering_rows(own, axes))


def scattering_tensor(partial, grid):
    rows, width = partial.shape
    parts = jnp.swapaxes(partial.reshape(1 << len(grid.x), 2, -1, width), 0, 1)
    return (yield from scattering_rows(parts.reshape(rows, width), grid.core + grid.x))


def gather_relative(values, axes):
    for axis in axes:
        values = jnp.concatenate([values, swap(values, axis)])
    return values


def gather_tensor(values, grid):
    rows, width = values.shape
    pieces = Transfers(gathering_rows(values, grid.core + grid.x)).finish()
    return jnp.swapaxes(pieces.reshape(2, -1, rows, width), 0, 1).reshape(-1, width)


def pair_steps(values, axes):
    for axis in axes:
        values = values + (yield values, axis)
    return values


NT = (((1,), (1,)), ((), ()))
TN = (((0,), (0,)), ((), ()))


def dot(left, right, dims=None):
    if dims is None:
        return jnp.dot(left, right, preferred_element_type=WIDE)
    return lax.dot_general(left, right, dims, preferred_element_type=WIDE)


def params(megabytes):
    return pltpu.CompilerParams(vmem_limit_bytes=megabytes << 20)


def cost(flops, moved):
    return pl.CostEstimate(flops=int(flops / EST), bytes_accessed=int(moved / EST), transcendentals=0)


def dispatch_kernel(order_ref, select_ref, rows_ref, out_ref):
    experts, capacity, width = out_ref.shape
    picked = dot(select_ref[0], rows_ref[0])
    out_ref[...] = picked.astype(LOW).reshape(experts, capacity, width)


def dispatch(order, select, rows, experts):
    blocks, slots, tokens = select.shape
    width = rows.shape[-1]
    capacity = slots // experts
    return pl.pallas_call(
        dispatch_kernel,
        grid_spec=pltpu.PrefetchScalarGridSpec(
            num_scalar_prefetch=1,
            grid=(blocks,),
            in_specs=[
                pl.BlockSpec((1, slots, tokens), lambda b, order: (b, 0, 0)),
                pl.BlockSpec((1, tokens, width), lambda b, order: (order[b], 0, 0)),
            ],
            out_specs=pl.BlockSpec((experts, capacity, width), lambda b, order: (0, b, 0)),
        ),
        out_shape=jax.ShapeDtypeStruct((experts, blocks * capacity, width), LOW),
        compiler_params=params(32),
        cost_estimate=cost(2 * blocks * slots * tokens * width, 2 * blocks * (slots + tokens) * width),
        name="dispatch",
    )(order, select, rows.reshape(blocks, tokens, width))


def row_tile(rows):
    return max(t for t in range(128, 513, 128) if rows % t == 0)


def grad_active_kernel(rows_ref, down_ref, out_ref):
    out_ref[0] = dot(rows_ref[0], down_ref[0], NT)


def grad_active(rows, expert_down):
    experts, count, width = rows.shape
    units = expert_down.shape[1]
    tile = row_tile(count)
    return pl.pallas_call(
        grad_active_kernel,
        grid=(experts, count // tile),
        in_specs=[
            pl.BlockSpec((1, tile, width), lambda e, r: (e, r, 0)),
            pl.BlockSpec((1, units, width), lambda e, r: (e, 0, 0)),
        ],
        out_specs=pl.BlockSpec((1, tile, units), lambda e, r: (e, r, 0)),
        out_shape=jax.ShapeDtypeStruct((experts, count, units), WIDE),
        compiler_params=params(32),
        cost_estimate=cost(2 * rows.size * units, 2 * rows.size),
        name="grad_active",
    )(rows, expert_down)


def hidden_kernel(rows_ref, up_ref, grad_ref, gate_ref, act_ref, pair_ref, gate_grad_ref):
    rows = rows_ref[0]
    gate_pre = dot(rows, up_ref[0, 0])
    upper = dot(rows, up_ref[0, 1])
    tile = rows.shape[0]
    gate = jnp.broadcast_to(gate_ref[0], (128, tile)).T[:, :1]
    sigma = jax.nn.sigmoid(gate_pre)
    silu = gate_pre * sigma
    active = silu * upper
    grad = grad_ref[0]
    gated = gate * grad
    act_ref[0] = (gate * active).astype(LOW)
    pair_ref[0, 0] = (gated * upper * (sigma * (1.0 + gate_pre * (1.0 - sigma)))).astype(LOW)
    pair_ref[0, 1] = (gated * silu).astype(LOW)
    gate_grad = jnp.sum(active * grad, axis=-1, keepdims=True)
    gate_grad_ref[0] = jnp.broadcast_to(gate_grad, (tile, 128)).T[:1]


def hidden_units(rows, expert_up, grads, gates):
    experts, count, width = rows.shape
    units = expert_up.shape[-1]
    tile = row_tile(count)
    return pl.pallas_call(
        hidden_kernel,
        grid=(experts, count // tile),
        in_specs=[
            pl.BlockSpec((1, tile, width), lambda e, r: (e, r, 0)),
            pl.BlockSpec((1, 2, width, units), lambda e, r: (e, 0, 0, 0)),
            pl.BlockSpec((1, tile, units), lambda e, r: (e, r, 0)),
            pl.BlockSpec((1, 1, tile), lambda e, r: (e, 0, r)),
        ],
        out_specs=[
            pl.BlockSpec((1, tile, units), lambda e, r: (e, r, 0)),
            pl.BlockSpec((1, 2, tile, units), lambda e, r: (e, 0, r, 0)),
            pl.BlockSpec((1, 1, tile), lambda e, r: (e, 0, r)),
        ],
        out_shape=[
            jax.ShapeDtypeStruct((experts, count, units), LOW),
            jax.ShapeDtypeStruct((experts, 2, count, units), LOW),
            jax.ShapeDtypeStruct((experts, 1, count), WIDE),
        ],
        compiler_params=params(40),
        cost_estimate=cost(4 * rows.size * units, 2 * rows.size),
        name="hidden_units",
    )(rows, expert_up, grads, gates)


def combine_kernel(transposed, experts, adds, extra, group_of, groups, *refs):
    lhs_ref, weight_ref, select_ref = refs[:3]
    refs = refs[3:]
    if extra:
        gate_ref, first_ref, refs = refs[0], refs[1], refs[2:]
    received, refs = (refs[:groups], refs[groups:]) if adds else ((None,) * groups, refs)
    outs, done_ref, rows = refs[:-2], refs[-2], refs[-1]
    step = pl.program_id(0)
    done_ref[...] = jnp.zeros_like(done_ref)
    blocks, slots, columns = rows.shape
    capacity = slots // experts
    group = select_ref.shape[0]
    pairs = lhs_ref.shape[1]
    many = math.gcd(blocks, 8)

    @pl.when(step < experts)
    def _():
        start = pl.multiple_of(step * capacity, capacity)
        for first in range(0, blocks, many):
            piece = pl.ds(first * capacity, many * capacity)
            total = None
            for i in range(pairs):
                term = dot(lhs_ref[0, i, piece, :], weight_ref[0, i], NT if transposed else None)
                total = term if total is None else total + term
            shape = (many, capacity, total.shape[-1])
            if extra:
                gates = jnp.broadcast_to(gate_ref[0, :, piece], (128, many * capacity)).T
                lane = lax.broadcasted_iota(jnp.int32, gates.shape, 1)
                gates = jnp.where(lane == first_ref[0] + step, gates, 0.0)
                rows[first : first + many, pl.ds(start, capacity), shape[-1] :] = gates.astype(
                    LOW
                ).reshape(many, capacity, 128)
            rows[first : first + many, pl.ds(start, capacity), : shape[-1]] = total.astype(
                LOW
            ).reshape(shape)

    @pl.when(step >= experts)
    def _():
        at = group_of(step) * group

        def put(out, more):
            for i in range(group):
                total = dot(select_ref[i], rows[at + i])
                if adds:
                    total = total + more[0, i].astype(WIDE)
                out[0, i] = total.astype(LOW)

        each = groups // len(outs)
        for place in range(groups):
            pl.when(step - experts == place)(
                functools.partial(put, outs[place // each], received[place])
            )


def combine(lhs, weight, select, received, at, columns, transposed, sizes, flip, after=(), gates=None):
    experts, pairs, count, units = lhs.shape
    blocks, tokens, slots = select.shape
    nx, ny, nz = sizes
    groups = nx * ny
    blocks //= 2
    count //= 2
    adds = received is not None
    part = 0 if adds else 1

    def group_of(s):
        place = jnp.clip(s - experts, 0, groups - 1)
        return place % nx * ny + place // nx if flip else place

    def expert_of(s):
        return jnp.minimum(s, experts - 1)

    if transposed:
        weight_spec = pl.BlockSpec((1, pairs, columns, units), lambda s: (expert_of(s), 0, at, 0))
    else:
        weight_spec = pl.BlockSpec((1, pairs, units, columns), lambda s: (expert_of(s), 0, 0, at))
    in_specs = [
        pl.BlockSpec((1, pairs, count, units), lambda s: (expert_of(s), 0, part, 0)),
        weight_spec,
        pl.BlockSpec((nz, tokens, slots), lambda s: (part * groups + group_of(s), 0, 0)),
    ]
    operands = [lhs, weight, select]
    if gates is not None:
        in_specs += [
            pl.BlockSpec((1, 1, count), lambda s: (expert_of(s), 0, part)),
            pl.BlockSpec(memory_space=pltpu.SMEM),
        ]
        operands += gates
        columns += 128
    if adds:
        in_specs += [pl.BlockSpec((1, nz, tokens, columns), lambda s: (0, 0, 0, 0))] * groups
        operands += received
        outs, half = 2, groups // 2
        place_of = lambda o, s: jnp.clip(s - experts - o * half, 0, half - 1)
    else:
        outs, half = groups, 1
        place_of = lambda o, s: 0
    out_specs = [
        pl.BlockSpec((1, nz, tokens, columns), functools.partial(lambda o, s: (place_of(o, s), 0, 0, 0), o))
        for o in range(outs)
    ]
    kernel = functools.partial(
        combine_kernel, transposed, experts, adds, gates is not None, group_of, groups
    )
    return pl.pallas_call(
        without(len(operands), len(after), kernel),
        grid=(experts + groups,),
        in_specs=in_specs + [pl.BlockSpec(memory_space=pl.ANY)] * len(after),
        out_specs=out_specs + [pl.BlockSpec((8, 128), lambda s: (0, 0))],
        out_shape=[jax.ShapeDtypeStruct((half, nz, tokens, columns), LOW)] * outs
        + [jax.ShapeDtypeStruct((8, 128), WIDE)],
        scratch_shapes=[pltpu.VMEM((blocks, slots, columns), LOW)],
        compiler_params=params(56),
        cost_estimate=cost(
            2 * lhs.size * columns + 2 * select.size * columns,
            2 * lhs.size + 2 * select.size + (12 if adds else 4) * blocks * tokens * columns,
        ),
        name="combine_own" if adds else "combine_other",
    )(*operands, *after)


def without(first, count, kernel):
    def run(*refs):
        kernel(*refs[:first], *refs[first + count :])

    return run


def spread(rows, columns, width):
    return (
        lax.broadcasted_iota(jnp.int32, (rows, width), 0),
        lax.broadcasted_iota(jnp.int32, (rows, width), 1) + columns,
    )


def turn(values, cosine, sine):
    return values * cosine + pltpu.roll(values, HEAD_DIM // 2, 1) * sine


def mean_last(values):
    return jnp.mean(values, axis=-1, keepdims=True)


def attention_kernel(tile, pre_ref, gain_ref, cos_ref, sin_ref, first_ref, out_refs, mixed_ref, lse_ref):
    length = pre_ref.shape[1]
    cosine, sine = cos_ref[...], sin_ref[...]
    for i in range(2):
        pre = pre_ref[i]
        inverse = lax.rsqrt(mean_last(pre * pre) + EPSILON)
        out_refs[i] = turn(pre * inverse * gain_ref[i], cosine, sine).astype(LOW)
    values = pre_ref[2].astype(LOW)
    out_refs[2] = values
    values_turned = values.T
    for start in range(0, length, tile):
        end = start + tile
        block = pl.ds(start, tile)
        scores = dot(out_refs[1, :end], out_refs[0, block], NT) * HEAD_DIM ** (-0.5)
        key, query = spread(end, start, tile)
        allowed = (key <= query) & (key >= first_ref[:, block])
        scores = jnp.where(allowed, scores, -1e30)
        top = jnp.max(scores, axis=0, keepdims=True)
        weights = jnp.exp(scores - top)
        total = jnp.sum(weights, axis=0, keepdims=True)
        lse_ref[0, :, block] = jnp.log(total) + top
        weights = (weights * (1.0 / total)).astype(LOW)
        mixed_ref[block, :] = dot(values_turned[:, :end], weights).T.astype(LOW)


def attention(projected, gains, cosine, sine, first):
    _, length, width = projected.shape
    tile = math.gcd(length, 256)
    head = lambda h: (0, 0, h)
    whole = lambda h: (0, 0)
    return pl.pallas_call(
        functools.partial(attention_kernel, tile),
        grid=(width // HEAD_DIM,),
        in_specs=[
            pl.BlockSpec((3, length, HEAD_DIM), head),
            pl.BlockSpec((2, 1, HEAD_DIM), head),
            pl.BlockSpec((length, HEAD_DIM), whole),
            pl.BlockSpec((length, HEAD_DIM), whole),
            pl.BlockSpec((1, length), whole),
        ],
        out_specs=[
            pl.BlockSpec((3, length, HEAD_DIM), head),
            pl.BlockSpec((length, HEAD_DIM), lambda h: (0, h)),
            pl.BlockSpec((1, 1, length), lambda h: (h, 0, 0)),
        ],
        out_shape=[
            jax.ShapeDtypeStruct(projected.shape, LOW),
            jax.ShapeDtypeStruct((length, width), LOW),
            jax.ShapeDtypeStruct((width // HEAD_DIM, 1, length), WIDE),
        ],
        compiler_params=params(48),
        cost_estimate=cost(6 * length * length * width, 40 * length * width),
        name="attention",
    )(projected, gains[:, None, :], cosine, sine, first)


def attention_back_kernel(
    tile,
    pre_ref,
    gain_ref,
    cos_ref,
    sin_ref,
    first_ref,
    low_ref,
    lse_ref,
    grad_ref,
    out_refs,
    gain_grad_ref,
    done_ref,
    query_grad,
    key_grad,
    value_grad,
):
    length = pre_ref.shape[1]
    scale = HEAD_DIM ** (-0.5)
    done_ref[...] = jnp.zeros_like(done_ref)
    keys_turned = low_ref[1].T
    for start in reversed(range(0, length, tile)):
        end = start + tile
        block = pl.ds(start, tile)
        queries, grads = low_ref[0, block], grad_ref[block, :]
        scores = dot(low_ref[1, :end], queries, NT) * scale
        key, query = spread(end, start, tile)
        allowed = (key <= query) & (key >= first_ref[:, block])
        weights = jnp.where(allowed, jnp.exp(scores - lse_ref[0, :, block]), 0.0)
        grad_weights = dot(low_ref[2, :end], grads, NT)
        mean = jnp.sum(grad_weights * weights, axis=0, keepdims=True)
        grad_scores = (weights * (grad_weights - mean)).astype(LOW)
        query_grad[block, :] = dot(keys_turned[:, :end], grad_scores).T
        key_term = dot(grad_scores, queries)
        value_term = dot(weights.astype(LOW), grads)
        if end == length:
            key_grad[...] = key_term
            value_grad[...] = value_term
        else:
            key_grad[:end] += key_term
            value_grad[:end] += value_term
    out_refs[2] = value_grad[...].astype(LOW)
    cosine, sine = cos_ref[...], sin_ref[...]
    for i, grad in enumerate((query_grad, key_grad)):
        grad = turn(grad[...] * scale, cosine, -sine)
        pre = pre_ref[i]
        inverse = lax.rsqrt(mean_last(pre * pre) + EPSILON)
        scaled = pre * inverse
        weighted = grad * gain_ref[i]
        out_refs[i] = (inverse * (weighted - scaled * mean_last(weighted * scaled))).astype(LOW)
        gain_grad_ref[i] = jnp.sum(grad * scaled, axis=0, keepdims=True)


def attention_back(projected, gains, cosine, sine, first, low, lse, grads, after=()):
    _, length, width = projected.shape
    tile = math.gcd(length, 256)
    head = lambda h: (0, 0, h)
    whole = lambda h: (0, 0)
    return pl.pallas_call(
        without(8, len(after), functools.partial(attention_back_kernel, tile)),
        grid=(width // HEAD_DIM,),
        in_specs=[
            pl.BlockSpec((3, length, HEAD_DIM), head),
            pl.BlockSpec((2, 1, HEAD_DIM), head),
            pl.BlockSpec((length, HEAD_DIM), whole),
            pl.BlockSpec((length, HEAD_DIM), whole),
            pl.BlockSpec((1, length), whole),
            pl.BlockSpec((3, length, HEAD_DIM), head),
            pl.BlockSpec((1, 1, length), lambda h: (h, 0, 0)),
            pl.BlockSpec((length, HEAD_DIM), lambda h: (0, h)),
        ]
        + [pl.BlockSpec(memory_space=pl.ANY)] * len(after),
        out_specs=[
            pl.BlockSpec((3, length, HEAD_DIM), head),
            pl.BlockSpec((2, 1, HEAD_DIM), head),
            pl.BlockSpec((8, 128), whole),
        ],
        out_shape=[
            jax.ShapeDtypeStruct(projected.shape, LOW),
            jax.ShapeDtypeStruct((2, 1, width), WIDE),
            jax.ShapeDtypeStruct((8, 128), WIDE),
        ],
        scratch_shapes=[pltpu.VMEM((length, HEAD_DIM), WIDE)] * 3,
        compiler_params=params(48),
        cost_estimate=cost(14 * length * length * width, 40 * length * width),
        name="attention_back",
    )(projected, gains[:, None, :], cosine, sine, first, low, lse, grads, *after)


def weight_grad_kernel(left_ref, right_ref, out_ref, done_ref):
    turned = left_ref[0].T
    for pair in range(out_ref.shape[1]):
        out_ref[0, pair] = dot(turned, right_ref[0, pair])
    done_ref[...] = jnp.zeros_like(done_ref)


def weight_grad(left, right, tile, first, last, into=None, after=()):
    experts, count, left_width = left.shape
    _, pairs, _, right_width = right.shape
    rest = ([] if into is None else [into]) + list(after)
    return pl.pallas_call(
        without(2, len(rest), weight_grad_kernel),
        grid=(last - first, left_width // tile),
        in_specs=[
            pl.BlockSpec((1, count, tile), lambda e, i: (e + first, 0, i)),
            pl.BlockSpec((1, pairs, count, right_width), lambda e, i: (e + first, 0, 0, 0)),
        ]
        + [pl.BlockSpec(memory_space=pl.ANY)] * len(rest),
        out_specs=[
            pl.BlockSpec((1, pairs, tile, right_width), lambda e, i: (e + first, 0, i, 0)),
            pl.BlockSpec((8, 128), lambda e, i: (0, 0)),
        ],
        out_shape=[
            jax.ShapeDtypeStruct((experts, pairs, left_width, right_width), WIDE),
            jax.ShapeDtypeStruct((8, 128), WIDE),
        ],
        input_output_aliases={} if into is None else {2: 0},
        compiler_params=params(48),
        cost_estimate=cost(
            2 * (last - first) * pairs * count * left_width * right_width,
            (2 * left.size + 2 * right.size + 4 * experts * pairs * left_width * right_width)
            * (last - first)
            // experts,
        ),
        name="weight_grad",
    )(left, right, *rest)


def shards(
    grid,
    hidden,
    segments,
    routes,
    attn_gain,
    qkv_weight,
    qk_gain,
    out_weight,
    moe_gain,
    router_weight,
    expert_up,
    expert_down,
    cotangent,
):
    tok_rows, width = hidden.shape
    length = segments.shape[0]
    local_experts = expert_up.shape[0]
    all_experts = router_weight.shape[1]
    nz, ny, nx = (1 << len(axes) for axes in (grid.z, grid.y, grid.x))
    n_tensor = nx * 2
    blocks = nz * ny * n_tensor
    capacity = max(2, 3 * length // (16 * n_tensor))
    capacity = -(-capacity // 16) * 16
    slots = local_experts * capacity
    expert_index = index_of(grid.expert)
    order_x = grid.x[::-1] + grid.y[::-1] + grid.z[::-1]
    order_y = grid.y[::-1] + grid.x[::-1] + grid.z[::-1]
    normed, inverse_attn = normalize(hidden, attn_gain)
    normed_all = gather_tensor(normed.astype(LOW), grid)
    cotangent_all = lax.all_gather(cotangent.astype(LOW), grid.all, axis=0, tiled=True)
    named = gather_relative(routes.T[None], (grid.core + order_x)[::-1])

    order = block_order(grid, grid.core + order_x)
    own_experts = expert_index * local_experts + jnp.arange(local_experts, dtype=jnp.int32)
    member = jnp.any(named[:, None, :, :] == own_experts[None, :, None, None], axis=2)
    token = jnp.arange(tok_rows, dtype=jnp.int32)
    earlier = (token[:, None] < token[None, :]).astype(LOW)
    rank = jnp.einsum("beu,ut->bet", member.astype(LOW), earlier, preferred_element_type=WIDE)
    rank = jnp.where(member, rank.astype(jnp.int32), -1)
    slot = jnp.arange(capacity, dtype=jnp.int32)
    chosen = rank[:, :, None, :] == slot[None, None, :, None]
    select = chosen.reshape(blocks, slots, tok_rows).astype(LOW)
    rank_back = jnp.swapaxes(rank, 1, 2)
    select_back = (rank_back[:, :, :, None] == slot).reshape(blocks, tok_rows, slots).astype(LOW)

    projected = jnp.einsum("td,cdf->ctf", normed_all, qkv_weight, preferred_element_type=WIDE)
    first_key = doc_starts(segments)
    cosine, sine = rope_tables(jnp.arange(length, dtype=jnp.int32) - first_key, HEAD_DIM // 2)
    first_key = first_key[None]
    heads_low, mixed, lse = attention(projected, qk_gain, cosine, sine, first_key)
    partial = jnp.dot(mixed, out_weight, preferred_element_type=WIDE).astype(LOW)
    attended = hidden + Transfers(scattering_tensor(partial, grid)).finish().astype(WIDE)
    moe_normed, inverse_moe = normalize(attended, moe_gain)
    routed_low = moe_normed.astype(LOW)
    routed_low, cotangent_all = lax.optimization_barrier((routed_low, cotangent_all))
    routed_all = lax.all_gather(routed_low, grid.all, axis=0, tiled=True)
    logits = jnp.dot(routed_low, router_weight, preferred_element_type=WIDE)
    shifted = jnp.exp(logits - jnp.max(logits, axis=-1, keepdims=True))
    probs = shifted / jnp.sum(shifted, axis=-1, keepdims=True)
    own_probs = probs.T[None]
    for axis in (grid.core + order_x)[::-1]:
        if axis in grid.expert:
            me = lax.axis_index(axis)
            count, columns, tokens = own_probs.shape
            parts = jnp.swapaxes(own_probs.reshape(count, 2, columns // 2, tokens), 0, 1)
            own_probs = jnp.concatenate(
                [pick(parts, me), swap(pick(parts, 1 - me), axis)]
            )
        else:
            own_probs = jnp.concatenate([own_probs, swap(own_probs, axis)])

    grad_slots = dispatch(order, select, cotangent_all, local_experts)
    grad_units = grad_active(grad_slots, expert_down)
    slot_gates = jnp.sum(
        jnp.where(chosen, own_probs[:, :, None, :], 0.0), axis=-1
    )
    slot_gates = jnp.swapaxes(slot_gates, 0, 1).reshape(local_experts, 1, blocks * capacity)
    row_slots = dispatch(order, select, routed_all, local_experts)
    gated_act, grad_pair, gate_grads = hidden_units(row_slots, expert_up, grad_units, slot_gates)

    sizes = (nx, ny, nz)
    chunk = 512
    act, down_weight = gated_act[:, None], expert_down[:, None]
    units = expert_up.shape[-1]

    def to_other(lhs, weight, transposed, at, flip, after, gates=None):
        parts = combine(
            lhs, weight, select_back, None, at, chunk, transposed, sizes, flip, after, gates
        )
        return parts[-1], [swap(part, "core") for part in parts[:-1]]

    def to_own(lhs, weight, transposed, at, flip, received, after, gates=None):
        return combine(
            lhs, weight, select_back, received, at, chunk, transposed, sizes, flip, after, gates
        )

    orders = (order_x, order_y, order_x, order_y)
    grads = (grad_pair, expert_up, True)
    outs = (act, down_weight, False)
    extra = [[gate_grads, (expert_index * local_experts)[None]], None, None, None]
    other, sent, own, rows = [None] * 4, [None] * 4, [None] * 4, [None] * 4

    def grad_other(i, before):
        done, sent[i] = to_other(*grads, i, i % 2 == 1, before, extra[i])
        return done

    def grad_own(i, before):
        *own, done = to_own(*grads, i, i % 2 == 1, sent[i], before, extra[i])
        rows[i] = Transfers(scattering(*own, orders[i]))
        return done

    o_sent, o_own, outputs = [None] * 4, [None] * 4, [None] * 4
    o_orders = (order_x, order_y, order_x, order_x)

    def out_other(i, before):
        done, o_sent[i] = to_other(*outs, i, i == 1, before)
        return done

    def out_own(i, before):
        *o_own[i], done = to_own(*outs, i, i == 1, o_sent[i], before)
        return done

    def out_start(i, done):
        outputs[i] = Transfers(scattering(*o_own[i], o_orders[i]), done)

    done = grad_other(0, ())
    done = grad_other(1, (done,))
    done = grad_own(0, (done,))
    done = grad_own(1, (done,))
    done = grad_other(2, (done,))
    done = grad_other(3, (done,))
    now = advance([rows[0]], done)
    done = grad_own(2, now)
    now = advance([rows[1]], done)
    done = grad_own(3, now)
    now = advance([rows[0]], done)
    done = out_other(0, now)
    done = out_other(1, (done,))
    now = advance([rows[0], rows[2]], done)
    done = out_own(0, now)
    now = advance([rows[1], rows[3], rows[0]], done)
    done = out_own(1, now)
    out_start(0, done)
    out_start(1, done)
    now = advance([rows[2], rows[1]], done)
    done = out_other(2, now)
    now = advance([rows[3], rows[1], rows[2]], done)
    done = out_other(3, now)
    advance([rows[2], rows[3]], done)
    advance([rows[3]], done)
    rows_back = jnp.concatenate([run.finish()[:, :chunk] for run in rows], axis=-1).astype(WIDE)
    grad_probs = rows[0].result[:, chunk : chunk + all_experts].astype(WIDE)

    chose = jnp.any(routes[:, :, None] == jnp.arange(all_experts, dtype=jnp.int32), axis=1)
    grad_probs = jnp.where(chose, grad_probs, 0.0)
    grad_logits = probs * (grad_probs - jnp.sum(probs * grad_probs, axis=-1, keepdims=True))
    logits_low = grad_logits.astype(LOW)
    router_grad = jnp.einsum("td,te->de", routed_low, logits_low, preferred_element_type=WIDE)
    grad_moe = jnp.einsum("te,de->td", logits_low, router_weight, preferred_element_type=WIDE)
    grad_moe = grad_moe + rows_back
    grad_attended, moe_gain_grad = norm_back(grad_moe, attended, inverse_moe, moe_gain)
    grad_attended = grad_attended + cotangent
    grad_low = grad_attended.astype(LOW)
    piece = gather_tensor(grad_low, grid)

    done = out_own(2, (grad_low,))
    done = out_own(3, (done,))
    now = advance([outputs[0], outputs[1]], done)
    piece = later(piece, done)
    out_start(2, done)
    out_start(3, done)

    sum_axes = grid.y + grid.z[::-1]
    grad_mixed = jnp.einsum("td,fd->tf", piece, out_weight, preferred_element_type=WIDE).astype(LOW)
    out_acc = jnp.einsum("tf,td->fd", mixed, piece, preferred_element_type=WIDE).astype(LOW)
    out_sum = Transfers(summing(out_acc, sum_axes))
    grad_proj, qk_gain_grad, done = attention_back(
        projected, qk_gain, cosine, sine, first_key, heads_low, lse, grad_mixed, (out_acc,) + now
    )
    qkv_sums = [
        Transfers(
            summing(
                jnp.einsum(
                    "td,tf->df", normed_all, grad_proj[i], preferred_element_type=WIDE
                ).astype(LOW),
                sum_axes,
            )
        )
        for i in (2, 0, 1)
    ]
    grad_normed = jnp.einsum(
        "ctf,cdf->td", grad_proj, qkv_weight, preferred_element_type=WIDE
    ).astype(LOW)
    normed_sum = Transfers(scattering_tensor(grad_normed, grid))
    gain_sum = Transfers(pair_steps(qk_gain_grad.reshape(2, -1), grid.expert))
    v_sum, q_sum, k_sum = qkv_sums
    now = (done, grad_normed) + tuple(run.sent for run in qkv_sums)
    gains = None
    waves = (
        (2, 0, [normed_sum, outputs[0], outputs[1], out_sum, v_sum]),
        (2, 0, [out_sum, v_sum, outputs[0], outputs[1], q_sum, k_sum, outputs[2]]),
        (2, 0, [normed_sum, out_sum, v_sum, q_sum, k_sum, outputs[0], outputs[1], gain_sum]),
        (2, 0, [out_sum, v_sum, q_sum, k_sum, outputs[3], outputs[2]]),
        (0, 4, [out_sum, v_sum, q_sum, k_sum, outputs[2], outputs[3], gain_sum]),
        (0, 4, [q_sum, k_sum, outputs[2], outputs[3]]),
        (0, 0, [outputs[3], gain_sum]),
    )

    def attention_norm_back(done):
        grad_normed = normed_sum.finish().astype(WIDE)
        grad_in, attn_gain_grad = norm_back(grad_normed, hidden, inverse_attn, attn_gain)
        both = jnp.stack([attn_gain_grad, moe_gain_grad])
        return grad_in + grad_attended, Transfers(pair_steps(both, grid.all[::-1]), done)

    up_left, down_left = list(range(local_experts)), list(range(local_experts))
    down_grad = up_grad = None
    for up_count, down_count, wave in waves:
        now_up, up_left = up_left[:up_count], up_left[up_count:]
        now_down, down_left = down_left[:down_count], down_left[down_count:]
        for e in now_up:
            up_grad, done = weight_grad(
                row_slots, grad_pair, 512, e, e + 1, up_grad, now
            )
            now = (done,)
        for e in now_down:
            down_grad, done = weight_grad(
                gated_act, grad_slots[:, None], units, e, e + 1, down_grad, now
            )
            now = (done,)
        now = advance(wave, done)
        if normed_sum.result is not None and gains is None:
            grad_hidden, gains = attention_norm_back(done)
        elif gains is not None:
            gains.advance(done)
    if gains is None:
        grad_hidden, gains = attention_norm_back(done)
    down_grad = down_grad.reshape(expert_down.shape)
    qkv_grad = jnp.stack([run.finish().astype(WIDE) for run in (q_sum, k_sum, v_sum)])
    out_grad = out_sum.finish().astype(WIDE)
    qk_gain_grad = gain_sum.finish()
    output = attended + jnp.concatenate([run.finish() for run in outputs], axis=-1).astype(WIDE)
    router_grad = lax.psum(router_grad, grid.all)
    attn_gain_grad, moe_gain_grad = gains.finish()
    return (
        output,
        grad_hidden,
        attn_gain_grad,
        qkv_grad,
        qk_gain_grad,
        out_grad,
        moe_gain_grad,
        router_grad,
        up_grad,
        down_grad,
    )


def solution(mesh):
    grid = Grid(mesh.shape["expert"], mesh.shape["tensor"])
    devices = Mesh(mesh.devices.reshape((2,) * len(grid.all)), grid.all)
    rows = P(grid.all, None)
    return jax.shard_map(
        functools.partial(shards, grid),
        mesh=devices,
        in_specs=(
            rows,
            P(grid.expert),
            rows,
            P(),
            P(None, None, grid.tensor),
            P(None, grid.tensor),
            P(grid.tensor, None),
            P(),
            P(),
            P(grid.expert, None, None, grid.tensor),
            P(grid.expert, grid.tensor, None),
            rows,
        ),
        out_specs=(
            rows,
            rows,
            P(),
            P(None, None, grid.tensor),
            P(None, grid.tensor),
            P(grid.tensor, None),
            P(),
            P(),
            P(grid.expert, None, None, grid.tensor),
            P(grid.expert, grid.tensor, None),
        ),
        check_vma=False,
    )
```
